256 devices in a mesh: section: 4 (over y_lo, core), fsdp: 64 (over x, z, y_hi).
Axes of the slice: x: 4, y: 4 (y_hi: 2, y_lo: 2; y = y_hi * 2 + y_lo), z: 8, core: 2. Of those that a mesh axis runs over, the one named last changes fastest.
Arguments:
- checkpoints: bfloat16 [4, 8192, 640], P('section', 'fsdp'), may hold values from -41 to 41
- cotangent: bfloat16 [8192, 640], P('fsdp'), may hold values from -6 to 6
- gains: float32 [4, 640], P('section'), may hold values from 0.25 to 1.75
- w_in: bfloat16 [4, 640, 2560], P('section', None, 'fsdp'), may hold values from -0.25 to 0.25
- w_out: bfloat16 [4, 2560, 640], P('section', 'fsdp'), may hold values from -0.125 to 0.125
- time_proj: bfloat16 [4, 256, 2560], P('section', None, 'fsdp'), may hold values from -0.375 to 0.375
- class_table: bfloat16 [4, 64, 2560], P('section', None, 'fsdp'), may hold values from -5 to 5
- timestep: int32 [8], replicated, may hold values from 0 to 999
- label: int32 [8], replicated, may hold values from 0 to 63
Outputs:
- section_input_grads: bfloat16 [4, 8192, 640], P('section', 'fsdp')
- w_in_grad: float32 [4, 640, 2560], P('section', None, 'fsdp')
- w_out_grad: float32 [4, 2560, 640], P('section', 'fsdp')
- gain_grad: float32 [4, 640], P('section')
The draws below stay inside these ranges and needn't reach their ends.
All inputs are finite; a program needn't handle non-finite values.
Results may differ from the reference program's by a relative error of at most 0.013.
Values may be sent and summed in bfloat16 or wider, within the bound.
No kernel may reach another device: no remote copies, remote signals or barrier semaphores. Data moves between devices by JAX's collectives and lax.ppermute only.
A program may use at most 128 MiB of HBM per device.

```python
import math
import jax
import jax.numpy as jnp
from jax import lax

C = 640
H = 2560
FREQ = 256
CLASSES = 64
TSTEPS = 1000
PIX = 1024
SECTIONS = 4
TOKENS = 8192
SAMPLES = 8


def draw_checkpoints(key, part):
    key = jax.random.fold_in(key, 11)
    key_base, key_rows, key_cols = jax.random.split(key, 3)
    full_shape = (SECTIONS, TOKENS, C)
    row_scale = jnp.exp(jax.random.uniform(key_rows, (SECTIONS, TOKENS, 1), jnp.float32, 0.0, math.log(10.0)))
    col_scale = jnp.exp(jax.random.uniform(key_cols, (SECTIONS, 1, C), jnp.float32, -0.7, 0.7))
    values = jnp.clip(jax.random.normal(key_base, full_shape, jnp.float32), -4.0, 4.0) * row_scale * col_scale * 0.5
    return values.astype(jnp.bfloat16)


def touch_ends(drawn, own_key, low, top_value):
    longest = drawn.shape.index(max(drawn.shape))
    spots = []
    for shift in (0, 1):
        where = [jax.random.randint(jax.random.fold_in(own_key, axis), (), 0, length) for axis, length in enumerate(drawn.shape)]
        where[longest] = (where[longest] + shift) % drawn.shape[longest]
        spots.append(tuple(where))
    return drawn.at[spots[0]].set(low).at[spots[1]].set(top_value)


def shard_levels(rng, dims, cuts, smallest, high):
    def one(position, blocks):
        heights = jax.random.uniform(jax.random.fold_in(jax.random.fold_in(rng, 6), position), (blocks,), jnp.float32, smallest / len(cuts), high / len(cuts))
        return jnp.repeat(jnp.exp(heights), dims[position] // blocks).reshape((-1,) + (1,) * (len(dims) - position - 1))

    level = one(*cuts[0])
    for cut in cuts[1:]:
        level = level * one(*cut)
    return level


def centred(rng, shape, scale, reach, shards=(), held_as=jnp.bfloat16):
    drawn = scale * jax.random.normal(rng, shape, jnp.float32)
    if shards:
        drawn = drawn * shard_levels(rng, shape, shards, -0.22, 0.18)
    return jnp.clip(drawn, -reach, reach).astype(held_as)


def setup_inputs(seed: int = 0) -> dict:
    streams_of = jax.random.split(jax.random.key(seed), 10)
    return {
        "checkpoints": draw_checkpoints(jax.random.fold_in(streams_of[9], 71), 0),
        "cotangent": centred(streams_of[1], (TOKENS, C), 1.0, 6.0, ((0, 64),)),
        "gains": jnp.clip(1.0 + 0.15 * jax.random.normal(streams_of[2], (SECTIONS, C), jnp.float32), 0.25, 1.75),
        "w_in": centred(streams_of[3], (SECTIONS, C, H), C ** -0.5, 0.25, ((0, 4), (2, 64))),
        "w_out": centred(streams_of[4], (SECTIONS, H, C), H ** -0.5, 0.125, ((0, 4), (1, 64))),
        "time_proj": centred(streams_of[5], (SECTIONS, FREQ, H), FREQ ** -0.5, 0.375, ((0, 4), (2, 64))),
        "class_table": centred(streams_of[6], (SECTIONS, CLASSES, H), 1.0, 5.0, ((0, 4), (2, 64))),
        "timestep": touch_ends(jax.random.randint(streams_of[7], (SAMPLES,), 0, TSTEPS), jax.random.fold_in(streams_of[7], 1), 0, TSTEPS - 1).astype(jnp.int32),
        "label": touch_ends(jax.random.randint(streams_of[8], (SAMPLES,), 0, CLASSES), jax.random.fold_in(streams_of[8], 1), 0, CLASSES - 1).astype(jnp.int32),
    }


def time_features(timestep, freq_width):
    half_width = freq_width // 2
    freq_rates = jnp.exp(-math.log(10000.0) * jnp.arange(half_width, dtype=jnp.float32) / half_width)
    angles = timestep.astype(jnp.float32)[:, None] * freq_rates[None, :]
    return jnp.concatenate([jnp.cos(angles), jnp.sin(angles)], axis=1).astype(jnp.bfloat16)

def reference(checkpoints, cotangent, gains, w_in, w_out, time_proj, class_table, timestep, label):
    time_feats = time_features(timestep, FREQ)
    class_picks = (label[:, None] == jnp.arange(CLASSES, dtype=jnp.int32)[None, :]).astype(jnp.bfloat16)
    grad_scale = float(TOKENS) ** (-0.5)
    grad_carry = cotangent
    input_list = []
    win_list = []
    wout_list = []
    gain_list = []
    for section_idx in reversed(range(SECTIONS)):
        inputs = checkpoints[section_idx].astype(jnp.float32)
        gain_row = gains[section_idx]
        mean_sq = lax.optimization_barrier(jnp.mean(inputs * inputs, axis=1, keepdims=True))
        rscale = lax.rsqrt(mean_sq + 1e-06)
        normed = (inputs * rscale * gain_row).astype(jnp.bfloat16)
        cond_small = jnp.dot(time_feats, time_proj[section_idx], preferred_element_type=jnp.float32) + jnp.dot(class_picks, class_table[section_idx], preferred_element_type=jnp.float32)
        cond_rows = jnp.repeat(cond_small, PIX, axis=0)
        pre = jnp.dot(normed, w_in[section_idx], preferred_element_type=jnp.float32) + cond_rows
        sigmoid_pre = jax.nn.sigmoid(pre)
        hidden = (pre * sigmoid_pre).astype(jnp.bfloat16)
        slope_pre = sigmoid_pre * (1.0 + pre * (1.0 - sigmoid_pre))
        hidden_grad = jnp.dot(grad_carry, w_out[section_idx].T, preferred_element_type=jnp.float32)
        pre_grad = (hidden_grad * slope_pre).astype(jnp.bfloat16)
        normed_grad = jnp.dot(pre_grad, w_in[section_idx].T, preferred_element_type=jnp.float32)
        scaled_grad = normed_grad * gain_row
        inner_mean = lax.optimization_barrier(jnp.mean(scaled_grad * inputs, axis=1, keepdims=True))
        grad_in = (grad_carry.astype(jnp.float32) + rscale * scaled_grad - inputs * (rscale * rscale * rscale) * inner_mean).astype(jnp.bfloat16)
        wout_list.append(jnp.dot(hidden.T, grad_carry, preferred_element_type=jnp.float32) * grad_scale)
        win_list.append(jnp.dot(normed.T, pre_grad, preferred_element_type=jnp.float32) * grad_scale)
        gain_list.append(lax.optimization_barrier(jnp.sum(normed_grad * inputs * rscale, axis=0)) * grad_scale)
        input_list.append(grad_in)
        grad_carry = grad_in
    input_list = input_list[::-1]
    win_list = win_list[::-1]
    wout_list = wout_list[::-1]
    gain_list = gain_list[::-1]
    return (jnp.stack(input_list), jnp.stack(win_list), jnp.stack(wout_list), jnp.stack(gain_list))
```

```python
import math

import jax
import jax.numpy as jnp
from jax import lax
from jax.sharding import Mesh, PartitionSpec as P

SAMPLES = 8
COLUMN = ("yl", "core", "z", "yh")
PLANE = ("x", "yl", "yh")
PEERS = 16
ALL = ("yl", "core", "x", "z", "yh")


def home_to_work(flip):
    pairs = []
    for i in range(64):
        sec, z2, z10, yh = i >> 4, (i >> 3) & 1, (i >> 1) & 3, i & 1
        pairs.append((i, (z10 << 4) | ((z2 ^ flip) << 3) | (sec << 1) | yh))
    return pairs


def work_to_home(flip):
    return [(j, i) for i, j in home_to_work(flip)]


def next_section():
    pairs = []
    for z in range(8):
        if z % 4:
            pairs.append((z, z - 1))
    return pairs


def across_cores(value):
    return lax.ppermute(value, "core", [(0, 1), (1, 0)])


def time_features(timestep, freq_width):
    half_width = freq_width // 2
    freq_rates = jnp.exp(
        -math.log(10000.0) * jnp.arange(half_width, dtype=jnp.float32) / half_width
    )
    angles = timestep.astype(jnp.float32)[:, None] * freq_rates[None, :]
    return jnp.concatenate([jnp.cos(angles), jnp.sin(angles)], axis=1).astype(jnp.bfloat16)


def contract_last(left_side, right_side):
    return lax.dot_general(
        left_side, right_side, (((1,), (1,)), ((), ())), preferred_element_type=jnp.float32
    )


def contract_first(left_side, right_side):
    return lax.dot_general(
        left_side, right_side, (((0,), (0,)), ((), ())), preferred_element_type=jnp.float32
    )


def matmul(left_side, right_side):
    return jnp.dot(left_side, right_side, preferred_element_type=jnp.float32)


def two_parts(value):
    high = lax.reduce_precision(value, 8, 7)
    return high.astype(jnp.bfloat16), (value - high).astype(jnp.bfloat16)


def gathered(chunk):
    copies = jnp.broadcast_to(chunk[None], (PEERS,) + chunk.shape)
    full = lax.all_to_all(copies, PLANE, 0, 0, tiled=True)
    return full.reshape(PEERS * chunk.shape[0], chunk.shape[1])


def on_device(checkpoints, cotangent, gains, w_in, w_out, time_proj, class_table, timestep, label):
    row_count, chan = checkpoints.shape[1:]
    own = w_in.shape[2]
    grad_scale = float(row_count * 64) ** (-0.5)
    section = lax.axis_index("z") % 4
    sample = 2 * lax.axis_index("x") + lax.axis_index("z") // 4

    time_feats = time_features(timestep, time_proj.shape[1])
    picks = (
        label[:, None] == jnp.arange(class_table.shape[1], dtype=jnp.int32)[None, :]
    ).astype(jnp.bfloat16)
    cond = lax.dot_general(
        time_proj[0], time_feats, (((0,), (1,)), ((), ())), preferred_element_type=jnp.float32
    ) + lax.dot_general(
        class_table[0], picks, (((0,), (1,)), ((), ())), preferred_element_type=jnp.float32
    )
    cond_high, cond_low = two_parts(cond)
    w_in_rows = jnp.concatenate(
        [
            w_in[0].T,
            cond_high,
            cond_low,
            jnp.zeros((own, 128 - 2 * SAMPLES), jnp.bfloat16),
        ],
        axis=1,
    )

    w_in_pair = jnp.concatenate(
        [lax.ppermute(w_in_rows, COLUMN, home_to_work(flip)) for flip in (0, 1)], axis=0
    )
    w_out_pair = jnp.concatenate(
        [lax.ppermute(w_out[0], COLUMN, home_to_work(flip)) for flip in (0, 1)], axis=0
    )
    x_rows = lax.ppermute(checkpoints[0], COLUMN, home_to_work(0))
    cot_rows = lax.ppermute(cotangent, COLUMN, home_to_work(0))
    gain_row = lax.ppermute(gains, COLUMN, home_to_work(0))

    w_in_near = gathered(w_in_pair)
    w_in_far = across_cores(w_in_near)
    w_out_near = gathered(w_out_pair)
    w_out_far = across_cores(w_out_near)

    inputs = x_rows.astype(jnp.float32)
    rscale = lax.rsqrt(jnp.mean(inputs * inputs, axis=1, keepdims=True) + 1e-06)
    normed = (inputs * rscale * gain_row).astype(jnp.bfloat16)
    lane = jnp.arange(128, dtype=jnp.int32)
    pick = ((lane == sample) | (lane == sample + SAMPLES)).astype(jnp.bfloat16)
    normed_wide = jnp.concatenate(
        [normed, jnp.broadcast_to(pick[None], (row_count, 128))], axis=1
    )

    def activation(weight):
        pre = contract_last(normed_wide, weight)
        sig = jax.nn.sigmoid(pre)
        return (pre * sig).astype(jnp.bfloat16), sig * (1.0 + pre * (1.0 - sig))

    hidden_near, slope_near = activation(w_in_near)
    hidden_far, slope_far = activation(w_in_far)

    def block_backward(grad):
        pg_near = (contract_last(grad, w_out_near) * slope_near).astype(jnp.bfloat16)
        pg_far = (contract_last(grad, w_out_far) * slope_far).astype(jnp.bfloat16)
        normed_grad = matmul(pg_near, w_in_near[:, :chan]) + matmul(pg_far, w_in_far[:, :chan])
        scaled = normed_grad * gain_row
        inner = jnp.mean(scaled * inputs, axis=1, keepdims=True)
        grad_in = (
            grad.astype(jnp.float32)
            + rscale * scaled
            - inputs * (rscale * rscale * rscale) * inner
        ).astype(jnp.bfloat16)
        return grad_in, normed_grad, pg_near, pg_far

    grad = jnp.where(section == 3, cot_rows, jnp.zeros_like(cot_rows))
    kept = grad
    for _ in range(3):
        grad = lax.ppermute(block_backward(grad)[0], "z", next_section())
        kept = kept + grad
    grad_in, normed_grad, pg_near, pg_far = block_backward(kept)

    grad_home = lax.ppermute(grad_in, COLUMN, work_to_home(0))
    gain_part = jnp.sum(normed_grad * inputs * rscale, axis=0, keepdims=True)
    gain_chip = gain_part + across_cores(gain_part)

    def chip_sum(left_near, left_far, right):
        far = contract_first(left_far, right).astype(jnp.bfloat16)
        near = contract_first(left_near, right)
        return near + across_cores(far).astype(jnp.float32)

    w_out_chip = chip_sum(hidden_near, hidden_far, kept).astype(jnp.bfloat16)
    w_in_chip = chip_sum(pg_near, pg_far, normed).astype(jnp.bfloat16)

    def plane_sum(chunks):
        parts = lax.all_to_all(chunks, PLANE, 0, 0, tiled=True)
        return jnp.sum(parts.astype(jnp.float32), axis=0)

    def sum_home(total):
        return sum(
            lax.ppermute(total[flip], COLUMN, work_to_home(flip)).astype(jnp.float32)
            for flip in (0, 1)
        )

    w_out_total = plane_sum(w_out_chip.reshape(PEERS, 2 * own, chan))
    gain_rows = jnp.concatenate(
        two_parts(gain_chip) + (jnp.zeros((6, chan), jnp.bfloat16),), axis=0
    )
    w_in_total = plane_sum(
        jnp.concatenate(
            [
                w_in_chip.reshape(PEERS, 2 * own, chan),
                jnp.broadcast_to(gain_rows[None], (PEERS, 8, chan)),
            ],
            axis=1,
        )
    )
    w_out_home = sum_home(w_out_total.reshape(2, own, chan).astype(jnp.bfloat16))
    gain_plane = w_in_total[2 * own : 2 * own + 1] + w_in_total[2 * own + 1 : 2 * own + 2]
    gain_rows_2 = jnp.concatenate(
        two_parts(gain_plane) + (jnp.zeros((6, chan), jnp.bfloat16),), axis=0
    )
    w_in_sum = w_in_total[: 2 * own].reshape(2, own, chan).astype(jnp.bfloat16)
    w_in_home = sum_home(
        jnp.concatenate([w_in_sum, jnp.broadcast_to(gain_rows_2[None], (2, 8, chan))], axis=1)
    )
    gain_home = (w_in_home[own : own + 1] + w_in_home[own + 1 : own + 2]) * grad_scale
    return (
        grad_home[None],
        (w_in_home[:own].T * grad_scale)[None],
        (w_out_home * grad_scale)[None],
        gain_home,
    )


def solution(mesh):
    fine = Mesh(mesh.devices.reshape(2, 2, 4, 8, 2), ALL)
    section, fsdp = ("yl", "core"), ("x", "z", "yh")
    in_specs = (
        P(section, fsdp, None),
        P(fsdp, None),
        P(section, None),
        P(section, None, fsdp),
        P(section, fsdp, None),
        P(section, None, fsdp),
        P(section, None, fsdp),
        P(),
        P(),
    )
    out_specs = (
        P(section, fsdp, None),
        P(section, None, fsdp),
        P(section, fsdp, None),
        P(section, None),
    )
    return jax.shard_map(
        on_device, mesh=fine, in_specs=in_specs, out_specs=out_specs, check_vma=False
    )
```

```python
import math

import jax
import jax.numpy as jnp
from jax import lax
from jax.experimental import pallas as pl
from jax.experimental.pallas import tpu as pltpu
from jax.sharding import Mesh, PartitionSpec as P

SAMPLES = 8
COLUMN = ("yl", "core", "z", "yh")
PLANE = ("x", "yl", "yh")
PEERS = 16
TILE = 640
VMEM_LIMIT = 28 << 20
ALL = ("yl", "core", "x", "z", "yh")


def home_to_work(flip):
    pairs = []
    for i in range(64):
        sec, z2, z10, yh = i >> 4, (i >> 3) & 1, (i >> 1) & 3, i & 1
        pairs.append((i, (z10 << 4) | ((z2 ^ flip) << 3) | (sec << 1) | yh))
    return pairs


def work_to_home(flip):
    return [(j, i) for i, j in home_to_work(flip)]


def next_section():
    pairs = []
    for z in range(8):
        if z % 4:
            pairs.append((z, z - 1))
    return pairs


def across_cores(value):
    return lax.ppermute(value, "core", [(0, 1), (1, 0)])


def time_features(timestep, freq_width):
    half_width = freq_width // 2
    freq_rates = jnp.exp(
        -math.log(10000.0) * jnp.arange(half_width, dtype=jnp.float32) / half_width
    )
    angles = timestep.astype(jnp.float32)[:, None] * freq_rates[None, :]
    return jnp.concatenate([jnp.cos(angles), jnp.sin(angles)], axis=1).astype(jnp.bfloat16)


def dot_rows(left_side, right_side):
    return lax.dot_general(
        left_side, right_side, (((1,), (1,)), ((), ())), preferred_element_type=jnp.float32
    )


def dot_plain(left_side, right_side):
    return lax.dot_general(
        left_side, right_side, (((1,), (0,)), ((), ())), preferred_element_type=jnp.float32
    )


def dot_first(left_side, right_side):
    return lax.dot_general(
        left_side, right_side, (((0,), (0,)), ((), ())), preferred_element_type=jnp.float32
    )


def two_parts(value):
    high = lax.reduce_precision(value, 8, 7)
    return high.astype(jnp.bfloat16), (value - high).astype(jnp.bfloat16)


def row_norm(x_ref):
    inputs = x_ref[...].astype(jnp.float32)
    rscale = lax.rsqrt(jnp.mean(inputs * inputs, axis=1, keepdims=True) + 1e-06)
    return rscale, inputs * rscale


def activation_kernel(x_ref, gain_ref, w_ref, cond_ref, normed_ref, hidden_ref, slope_ref):
    _, unit = row_norm(x_ref)
    normed = (unit * gain_ref[...]).astype(jnp.bfloat16)
    normed_ref[...] = normed
    for at in range(0, w_ref.shape[0], TILE):
        cols = pl.ds(at, TILE)
        pre = dot_rows(normed, w_ref[cols, :]) + cond_ref[:, cols]
        sig = jax.nn.sigmoid(pre)
        hidden_ref[:, cols] = (pre * sig).astype(jnp.bfloat16)
        slope_ref[:, cols] = sig * (1.0 + pre * (1.0 - sig))


def turn_body(g_ref, x_ref, gain_ref, halves, keep):
    grad = g_ref[...]
    total = None
    for w_in_ref, w_out_ref, slope_ref, pg_ref in halves:
        for at in range(0, w_in_ref.shape[0], TILE):
            cols = pl.ds(at, TILE)
            pre_grad = (dot_rows(grad, w_out_ref[cols, :]) * slope_ref[:, cols]).astype(
                jnp.bfloat16
            )
            if keep:
                pg_ref[:, cols] = pre_grad
            term = dot_plain(pre_grad, w_in_ref[cols, :])
            total = term if total is None else total + term
    rscale, unit = row_norm(x_ref)
    scaled = total * gain_ref[...]
    inner = jnp.mean(scaled * unit, axis=1, keepdims=True)
    grad_in = grad.astype(jnp.float32) + rscale * (scaled - unit * inner)
    return grad_in.astype(jnp.bfloat16), total * unit


def turn_kernel(g, x, gain, wi_n, wo_n, sl_n, wi_f, wo_f, sl_f, out):
    halves = ((wi_n, wo_n, sl_n, None), (wi_f, wo_f, sl_f, None))
    out[...] = turn_body(g, x, gain, halves, False)[0]


def last_turn_kernel(
    g, x, gain, wi_n, wo_n, sl_n, wi_f, wo_f, sl_f, normed, out, gain_out, pg_n, pg_f, far_out
):
    halves = ((wi_n, wo_n, sl_n, pg_n), (wi_f, wo_f, sl_f, pg_f))
    grad_in, terms = turn_body(g, x, gain, halves, True)
    out[...] = grad_in
    gain_out[...] = jnp.sum(terms, axis=0, keepdims=True)
    for at in range(0, pg_f.shape[1], TILE):
        cols = pl.ds(at, TILE)
        far_out[cols, :] = dot_first(pg_f[:, cols], normed[...]).astype(jnp.bfloat16)


def outer_kernel(left, right, out):
    for at in range(0, left.shape[1], TILE):
        cols = pl.ds(at, TILE)
        out[cols, :] = dot_first(left[:, cols], right[...]).astype(jnp.bfloat16)


def near_kernel(pg, normed, in_far, hidden, grad, out_far, sums):
    peers, rows = sums.shape[0], sums.shape[1] // 2
    span = 8
    for first, (left, right, far) in enumerate(((pg, normed, in_far), (hidden, grad, out_far))):
        for at in range(0, peers, span):
            cols = pl.ds(at * rows, span * rows)
            total = dot_first(left[:, cols], right[...]) + far[cols, :].astype(jnp.float32)
            total = total.astype(jnp.bfloat16)
            for k in range(span):
                sums[at + k, pl.ds(first * rows, rows), :] = total[k * rows : (k + 1) * rows, :]


def kernel(body, outs, flops=0):
    whole = pl.BlockSpec(memory_space=pltpu.VMEM)
    shapes = [jax.ShapeDtypeStruct(*out) for out in outs]

    def call(*operands):
        result = pl.pallas_call(
            body,
            out_shape=shapes,
            in_specs=[whole] * len(operands),
            out_specs=[whole] * len(shapes),
            compiler_params=pltpu.CompilerParams(vmem_limit_bytes=VMEM_LIMIT),
            cost_estimate=pl.CostEstimate(flops=flops, bytes_accessed=4 << 20, transcendentals=0),
        )(*operands)
        return result if len(shapes) > 1 else result[0]

    return call


def on_device(checkpoints, cotangent, gains, w_in, w_out, time_proj, class_table, timestep, label):
    rows, chan = checkpoints.shape[1:]
    own = w_in.shape[2]
    half = PEERS * 2 * own
    grad_scale = float(rows * 64) ** (-0.5)
    section = lax.axis_index("z") % 4
    sample = 2 * lax.axis_index("x") + lax.axis_index("z") // 4
    bf16, f32 = jnp.bfloat16, jnp.float32

    time_feats = time_features(timestep, time_proj.shape[1])
    picks = (
        label[:, None] == jnp.arange(class_table.shape[1], dtype=jnp.int32)[None, :]
    ).astype(bf16)
    cond = dot_plain(time_feats, time_proj[0]) + dot_plain(picks, class_table[0])
    cond_row = jnp.concatenate([part.reshape(1, -1) for part in two_parts(cond)], axis=1)
    shard = jnp.concatenate(
        [w_in[0].T, w_out[0], cond_row, jnp.zeros((7, chan), bf16)], axis=0
    )

    one, two = (lax.ppermute(shard, COLUMN, home_to_work(flip)) for flip in (0, 1))
    chunk = jnp.concatenate(
        [
            one[:own],
            two[:own],
            one[own : 2 * own],
            two[own : 2 * own],
            one[2 * own : 2 * own + 1],
            two[2 * own : 2 * own + 1],
            jnp.zeros((6, chan), bf16),
        ],
        axis=0,
    )
    full = lax.all_to_all(
        jnp.broadcast_to(chunk[None], (PEERS,) + chunk.shape), PLANE, 0, 0, tiled=True
    )
    x_rows = lax.ppermute(checkpoints[0], COLUMN, home_to_work(0))
    cot_rows = lax.ppermute(cotangent, COLUMN, home_to_work(0))
    gain_row = lax.ppermute(gains, COLUMN, home_to_work(0))

    wi_n = full[:, : 2 * own].reshape(half, chan)
    wi_f = across_cores(wi_n)
    wo_n = full[:, 2 * own : 4 * own].reshape(half, chan)
    wo_f = across_cores(wo_n)
    conds = full[:, 4 * own : 4 * own + 2].astype(f32).reshape(PEERS * 2, 2, SAMPLES, own)
    cond_n = lax.dynamic_index_in_dim(conds, sample, 2, False).sum(axis=1).reshape(1, half)
    cond_f = across_cores(cond_n)

    flops = 2 * rows * half * chan
    activate = kernel(
        activation_kernel, [((rows, chan), bf16), ((rows, half), bf16), ((rows, half), f32)], flops
    )
    normed, hidden_n, slope_n = activate(x_rows, gain_row, wi_n, cond_n)
    _, hidden_f, slope_f = activate(x_rows, gain_row, wi_f, cond_f)

    turn = kernel(turn_kernel, [((rows, chan), bf16)], 4 * flops)
    held = (x_rows, gain_row, wi_n, wo_n, slope_n, wi_f, wo_f, slope_f)
    grad = jnp.where(section == 3, cot_rows, jnp.zeros_like(cot_rows))
    kept = grad
    for _ in range(3):
        grad = lax.ppermute(turn(grad, *held), "z", next_section())
        kept = kept + grad

    far_out = kernel(outer_kernel, [((half, chan), bf16)], flops)(hidden_f, kept)
    recv_out = across_cores(far_out)
    last_turn = kernel(
        last_turn_kernel,
        [
            ((rows, chan), bf16),
            ((1, chan), f32),
            ((rows, half), bf16),
            ((rows, half), bf16),
            ((half, chan), bf16),
        ],
        5 * flops,
    )
    grad_in, gain_part, pg_n, _, far_in = last_turn(kept, *held, normed)
    recv_in = across_cores(far_in)
    sums = kernel(near_kernel, [((PEERS, 4 * own, chan), bf16)], 2 * flops)(
        pg_n, normed, recv_in, hidden_n, kept, recv_out
    )
    parts = lax.all_to_all(sums, PLANE, 0, 0, tiled=True)

    grad_home = lax.ppermute(grad_in, COLUMN, work_to_home(0))
    gain_sum = gain_part
    for axis, size, bit in (("core", 2, 1), ("x", 4, 1), ("x", 4, 2), ("yl", 2, 1), ("yh", 2, 1), ("z", 8, 4)):
        gain_sum = gain_sum + lax.ppermute(gain_sum, axis, [(i, i ^ bit) for i in range(size)])
    gain_home = lax.ppermute(gain_sum, COLUMN, work_to_home(0)) * grad_scale

    total = jnp.sum(parts.astype(f32), axis=0).astype(bf16).reshape(2, 2, own, chan)
    home = sum(
        lax.ppermute(total[:, flip], COLUMN, work_to_home(flip)).astype(f32) for flip in (0, 1)
    )
    return (
        grad_home[None],
        (home[0].T * grad_scale)[None],
        (home[1] * grad_scale)[None],
        gain_home,
    )


def solution(mesh):
    fine = Mesh(mesh.devices.reshape(2, 2, 4, 8, 2), ALL)
    section, fsdp = ("yl", "core"), ("x", "z", "yh")
    in_specs = (
        P(section, fsdp, None),
        P(fsdp, None),
        P(section, None),
        P(section, None, fsdp),
        P(section, fsdp, None),
        P(section, None, fsdp),
        P(section, None, fsdp),
        P(),
        P(),
    )
    out_specs = (
        P(section, fsdp, None),
        P(section, None, fsdp),
        P(section, fsdp, None),
        P(section, None),
    )
    return jax.shard_map(
        on_device, mesh=fine, in_specs=in_specs, out_specs=out_specs, check_vma=False
    )
```

```python
import math

import jax
import jax.numpy as jnp
from jax import lax
from jax.experimental import pallas as pl
from jax.experimental.pallas import tpu as pltpu
from jax.sharding import Mesh, PartitionSpec as P

SAMPLES = 8
COLUMN = ("yl", "core", "z", "yh")
PLANE = ("yl", "core", "x", "yh")
SIDE = 4
TILE = 640
PAD = 16
VMEM_LIMIT = 28 << 20
ALL = ("yl", "core", "x", "z", "yh")


def home_to_work(flip):
    pairs = []
    for i in range(64):
        sec, z2, z10, yh = i >> 4, (i >> 3) & 1, (i >> 1) & 3, i & 1
        pairs.append((i, (z10 << 4) | ((z2 ^ flip) << 3) | (sec << 1) | yh))
    return pairs


def work_to_home(flip):
    return [(j, i) for i, j in home_to_work(flip)]


def next_section():
    pairs = []
    for z in range(8):
        if z % 4:
            pairs.append((z, z - 1))
    return pairs


def along(stage, shift):
    pairs = []
    for i in range(32):
        yl, core, x, yh = i >> 4, (i >> 3) & 1, (i >> 1) & 3, i & 1
        if (core == 0) == (stage == 1):
            x = (x + shift) % SIDE
        else:
            y = (2 * yh + yl + shift) % SIDE
            yl, yh = y % 2, y // 2
        pairs.append((i, (yl << 4) | (core << 3) | (x << 1) | yh))
    return pairs


def across_cores(value):
    return lax.ppermute(value, "core", [(0, 1), (1, 0)])


def time_features(timestep, freq_width):
    half_width = freq_width // 2
    freq_rates = jnp.exp(
        -math.log(10000.0) * jnp.arange(half_width, dtype=jnp.float32) / half_width
    )
    angles = timestep.astype(jnp.float32)[:, None] * freq_rates[None, :]
    return jnp.concatenate([jnp.cos(angles), jnp.sin(angles)], axis=1).astype(jnp.bfloat16)


def dot_rows(left_side, right_side):
    return lax.dot_general(
        left_side, right_side, (((1,), (1,)), ((), ())), preferred_element_type=jnp.float32
    )


def dot_plain(left_side, right_side):
    return lax.dot_general(
        left_side, right_side, (((1,), (0,)), ((), ())), preferred_element_type=jnp.float32
    )


def dot_first(left_side, right_side):
    return lax.dot_general(
        left_side, right_side, (((0,), (0,)), ((), ())), preferred_element_type=jnp.float32
    )


def two_parts(value):
    high = lax.reduce_precision(value, 8, 7)
    return high.astype(jnp.bfloat16), (value - high).astype(jnp.bfloat16)


def row_norm(x_ref):
    inputs = x_ref[...].astype(jnp.float32)
    rscale = lax.rsqrt(jnp.mean(inputs * inputs, axis=1, keepdims=True) + 1e-06)
    return rscale, inputs * rscale


def activation_kernel(
    x_ref, gain_ref, select_ref, b0, b1, b2, b3, w_in_ref, w_out_ref, normed_ref, hidden_ref, slope_ref
):
    blocks = (b0, b1, b2, b3)
    step = b0.shape[0] // SIDE
    rows = (step - PAD) // 2
    half = 2 * SIDE * SIDE * (rows // 2)
    extras = []
    for n, block in enumerate(blocks):
        for k in range(SIDE):
            to = pl.ds((n * SIDE + k) * rows, rows)
            w_in_ref[to, :] = block[pl.ds(k * step, rows), :]
            w_out_ref[to, :] = block[pl.ds(k * step + rows, rows), :]
            extras.append(block[pl.ds(k * step + 2 * rows, PAD), :])
    _, unit = row_norm(x_ref)
    normed = (unit * gain_ref[...]).astype(jnp.bfloat16)
    normed_ref[...] = normed
    extras = jnp.concatenate(extras, axis=0)
    for at in range(0, half, TILE):
        cols = pl.ds(at, TILE)
        spread = dot_plain(extras, select_ref[:, cols])
        line = lax.broadcasted_iota(jnp.int32, spread.shape, 0)
        shard = (lax.broadcasted_iota(jnp.int32, spread.shape, 1) + at) // (rows // 2)
        mine = (line // PAD * 2 + line % PAD == shard) & (line % PAD < 2)
        cond = jnp.sum(jnp.where(mine, spread, 0.0), axis=0, keepdims=True)
        pre = dot_rows(normed, w_in_ref[cols, :]) + cond
        sig = jax.nn.sigmoid(pre)
        hidden_ref[:, cols] = (pre * sig).astype(jnp.bfloat16)
        slope_ref[:, cols] = sig * (1.0 + pre * (1.0 - sig))


def turn_body(g_ref, x_ref, gain_ref, halves, keep):
    grad = g_ref[...]
    total = None
    for w_in_ref, w_out_ref, slope_ref, pg_ref in halves:
        for at in range(0, w_in_ref.shape[0], TILE):
            cols = pl.ds(at, TILE)
            pre_grad = (dot_rows(grad, w_out_ref[cols, :]) * slope_ref[:, cols]).astype(
                jnp.bfloat16
            )
            if keep:
                pg_ref[:, cols] = pre_grad
            term = dot_plain(pre_grad, w_in_ref[cols, :])
            total = term if total is None else total + term
    rscale, unit = row_norm(x_ref)
    scaled = total * gain_ref[...]
    inner = jnp.mean(scaled * unit, axis=1, keepdims=True)
    grad_in = grad.astype(jnp.float32) + rscale * (scaled - unit * inner)
    return grad_in.astype(jnp.bfloat16), total * unit


def turn_kernel(g, x, gain, wi_n, wo_n, sl_n, wi_f, wo_f, sl_f, out):
    halves = ((wi_n, wo_n, sl_n, None), (wi_f, wo_f, sl_f, None))
    out[...] = turn_body(g, x, gain, halves, False)[0]


def last_turn_kernel(
    g, x, gain, wi_n, wo_n, sl_n, wi_f, wo_f, sl_f, normed, out, gain_out, pg_n, pg_f, far_out
):
    halves = ((wi_n, wo_n, sl_n, pg_n), (wi_f, wo_f, sl_f, pg_f))
    grad_in, terms = turn_body(g, x, gain, halves, True)
    out[...] = grad_in
    gain_out[...] = jnp.sum(terms, axis=0, keepdims=True)
    for at in range(0, pg_f.shape[1], TILE):
        cols = pl.ds(at, TILE)
        far_out[cols, :] = dot_first(pg_f[:, cols], normed[...]).astype(jnp.bfloat16)


def outer_kernel(left, right, out):
    for at in range(0, left.shape[1], TILE):
        cols = pl.ds(at, TILE)
        out[cols, :] = dot_first(left[:, cols], right[...]).astype(jnp.bfloat16)


def high_low_rows(value):
    line = lax.broadcasted_iota(jnp.int32, (PAD, value.shape[1]), 0)
    high = value.astype(jnp.bfloat16).astype(jnp.float32)
    rows = jnp.where(line == 0, high, jnp.where(line == 1, value - high, 0.0))
    return rows.astype(jnp.bfloat16)


def near_kernel(pg, normed, in_far, hidden, grad, out_far, gain_here, gain_there, *sums):
    rows = (sums[0].shape[0] - PAD) // SIDE // 2
    for first, (left, right, far) in enumerate(((pg, normed, in_far), (hidden, grad, out_far))):
        for at in range(0, left.shape[1], TILE):
            cols = pl.ds(at, TILE)
            total = dot_first(left[:, cols], right[...]) + far[cols, :].astype(jnp.float32)
            total = total.astype(jnp.bfloat16)
            for k in range(TILE // rows):
                peer = at // rows + k
                to = pl.ds((peer % SIDE * 2 + first) * rows, rows)
                sums[peer // SIDE][to, :] = total[k * rows : (k + 1) * rows, :]
    gain = high_low_rows(gain_here[...] + gain_there[...])
    for out in sums:
        out[pl.ds(out.shape[0] - PAD, PAD), :] = gain


def stage_sum_kernel(s0, s1, s2, s3, *outs):
    rows = outs[0].shape[0] - PAD
    for k, out in enumerate(outs):
        cut = pl.ds(k * rows, rows)
        total = sum(s[cut, :].astype(jnp.float32) for s in (s0, s1, s2, s3))
        out[pl.ds(0, rows), :] = total.astype(jnp.bfloat16)
    tail = pl.ds(s0.shape[0] - PAD, PAD)
    total = sum(s[tail, :].astype(jnp.float32) for s in (s0, s1, s2, s3))
    gain = high_low_rows(jnp.sum(total, axis=0, keepdims=True))
    for out in outs:
        out[pl.ds(rows, PAD), :] = gain


def kernel(body, outs, flops=0):
    whole = pl.BlockSpec(memory_space=pltpu.VMEM)
    shapes = [jax.ShapeDtypeStruct(*out) for out in outs]

    def call(*operands):
        result = pl.pallas_call(
            body,
            out_shape=shapes,
            in_specs=[whole] * len(operands),
            out_specs=[whole] * len(shapes),
            compiler_params=pltpu.CompilerParams(vmem_limit_bytes=VMEM_LIMIT),
            cost_estimate=pl.CostEstimate(flops=flops, bytes_accessed=4 << 20, transcendentals=0),
        )(*operands)
        return result if len(shapes) > 1 else result[0]

    return call


def on_device(checkpoints, cotangent, gains, w_in, w_out, time_proj, class_table, timestep, label):
    rows, chan = checkpoints.shape[1:]
    own = w_in.shape[2]
    half = SIDE * SIDE * 2 * own
    grad_scale = float(rows * 64) ** (-0.5)
    section = lax.axis_index("z") % 4
    sample = 2 * lax.axis_index("x") + lax.axis_index("z") // 4
    bf16, f32 = jnp.bfloat16, jnp.float32

    time_feats = time_features(timestep, time_proj.shape[1])
    picks = (
        label[:, None] == jnp.arange(class_table.shape[1], dtype=jnp.int32)[None, :]
    ).astype(bf16)
    cond = dot_plain(time_feats, time_proj[0]) + dot_plain(picks, class_table[0])
    cond_row = jnp.concatenate([part.reshape(1, -1) for part in two_parts(cond)], axis=1)
    shard = jnp.concatenate(
        [w_in[0].T, w_out[0], cond_row, jnp.zeros((7, chan), bf16)], axis=0
    )

    one, two = (lax.ppermute(shard, COLUMN, home_to_work(flip)) for flip in (0, 1))
    x_rows = lax.ppermute(checkpoints[0], COLUMN, home_to_work(0))
    cot_rows = lax.ppermute(cotangent, COLUMN, home_to_work(0))
    gain_row = lax.ppermute(gains, COLUMN, home_to_work(0))
    one, two, x_rows, cot_rows, gain_row = lax.optimization_barrier(
        (one, two, x_rows, cot_rows, gain_row)
    )
    chunk = jnp.concatenate(
        [
            one[:own],
            two[:own],
            one[own : 2 * own],
            two[own : 2 * own],
            one[2 * own : 2 * own + 1],
            two[2 * own : 2 * own + 1],
            jnp.zeros((PAD - 2, chan), bf16),
        ],
        axis=0,
    )
    quarter = jnp.concatenate(
        [chunk] + [lax.ppermute(chunk, PLANE, along(1, k)) for k in range(1, SIDE)], axis=0
    )
    near = [quarter] + [lax.ppermute(quarter, PLANE, along(2, k)) for k in range(1, SIDE)]
    far = [across_cores(block) for block in near]

    entry = jnp.arange(chan, dtype=jnp.int32)[:, None]
    hidden_col = jnp.arange(half, dtype=jnp.int32)[None, :]
    select = (
        (entry % own == hidden_col % own) & (entry // own % SAMPLES == sample)
    ).astype(bf16)

    flops = 2 * rows * half * chan
    activate = kernel(
        activation_kernel,
        [
            ((half, chan), bf16),
            ((half, chan), bf16),
            ((rows, chan), bf16),
            ((rows, half), bf16),
            ((rows, half), f32),
        ],
        2 * flops,
    )
    wi_n, wo_n, normed, hidden_n, slope_n = activate(x_rows, gain_row, select, *near)
    wi_f, wo_f, _, hidden_f, slope_f = activate(x_rows, gain_row, select, *far)

    turn = kernel(turn_kernel, [((rows, chan), bf16)], 4 * flops)
    held = (x_rows, gain_row, wi_n, wo_n, slope_n, wi_f, wo_f, slope_f)
    grad = jnp.where(section == 3, cot_rows, jnp.zeros_like(cot_rows))
    kept = grad
    for _ in range(3):
        grad = lax.ppermute(turn(grad, *held), "z", next_section())
        kept = kept + grad

    far_out = kernel(outer_kernel, [((half, chan), bf16)], flops)(hidden_f, kept)
    recv_out = across_cores(far_out)
    last_turn = kernel(
        last_turn_kernel,
        [
            ((rows, chan), bf16),
            ((1, chan), f32),
            ((rows, half), bf16),
            ((rows, half), bf16),
            ((half, chan), bf16),
        ],
        5 * flops,
    )
    grad_in, gain_part, pg_n, _, far_in = last_turn(kept, *held, normed)
    recv_in = across_cores(far_in)
    gain_there = across_cores(gain_part)
    sums = kernel(near_kernel, [((SIDE * 4 * own + PAD, chan), bf16)] * SIDE, 2 * flops)(
        pg_n, normed, recv_in, hidden_n, kept, recv_out, gain_part, gain_there
    )
    grad_home = lax.ppermute(grad_in, COLUMN, work_to_home(0))

    parts = [sums[0]] + [
        lax.ppermute(sums[k], PLANE, along(2, SIDE - k)) for k in range(1, SIDE)
    ]
    sums = kernel(stage_sum_kernel, [((4 * own + PAD, chan), bf16)] * SIDE)(*parts)
    parts = [sums[0]] + [
        lax.ppermute(sums[k], PLANE, along(1, SIDE - k)) for k in range(1, SIDE)
    ]
    total = sum(part.astype(f32) for part in parts)
    gain_lines = list(two_parts(total[4 * own : 4 * own + 1] + total[4 * own + 1 : 4 * own + 2]))
    gain_lines.append(jnp.zeros((6, chan), bf16))
    total = total.astype(bf16)
    home = sum(
        lax.ppermute(
            jnp.concatenate(
                [
                    total[flip * own : (flip + 1) * own],
                    total[(2 + flip) * own : (3 + flip) * own],
                    *gain_lines,
                ],
                axis=0,
            ),
            COLUMN,
            work_to_home(flip),
        ).astype(f32)
        for flip in (0, 1)
    )
    return (
        grad_home[None],
        (home[:own].T * grad_scale)[None],
        (home[own : 2 * own] * grad_scale)[None],
        (home[2 * own : 2 * own + 1] + home[2 * own + 1 : 2 * own + 2]) * grad_scale,
    )


def solution(mesh):
    fine = Mesh(mesh.devices.reshape(2, 2, 4, 8, 2), ALL)
    section, fsdp = ("yl", "core"), ("x", "z", "yh")
    in_specs = (
        P(section, fsdp, None),
        P(fsdp, None),
        P(section, None),
        P(section, None, fsdp),
        P(section, fsdp, None),
        P(section, None, fsdp),
        P(section, None, fsdp),
        P(),
        P(),
    )
    out_specs = (
        P(section, fsdp, None),
        P(section, None, fsdp),
        P(section, fsdp, None),
        P(section, None),
    )
    return jax.shard_map(
        on_device, mesh=fine, in_specs=in_specs, out_specs=out_specs, check_vma=False
    )
```

```python
import math

import jax
import jax.numpy as jnp
from jax import lax
from jax.experimental import pallas as pl
from jax.experimental.pallas import tpu as pltpu
from jax.sharding import Mesh, PartitionSpec as P

SAMPLES = 8
COLUMN = ("yl", "core", "z", "yh")
PLANE = ("yl", "core", "x", "yh")
SIDE = 4
PAD = 16
LINES = 8
VMEM_LIMIT = 28 << 20
ALL = ("yl", "core", "x", "z", "yh")


def home_to_work(flip):
    pairs = []
    for i in range(64):
        sec, z2, z10, yh = i >> 4, (i >> 3) & 1, (i >> 1) & 3, i & 1
        pairs.append((i, (z10 << 4) | ((z2 ^ flip) << 3) | (sec << 1) | yh))
    return pairs


def work_to_home(flip):
    return [(j, i) for i, j in home_to_work(flip)]


def next_section():
    return [(z, (z - 1) % 8) for z in range(8)]


def along(stage, shift):
    pairs = []
    for i in range(32):
        yl, core, x, yh = i >> 4, (i >> 3) & 1, (i >> 1) & 3, i & 1
        if (core == 0) == (stage == 1):
            x = (x + shift) % SIDE
        else:
            y = (2 * yh + yl + shift) % SIDE
            yl, yh = y % 2, y // 2
        pairs.append((i, (yl << 4) | (core << 3) | (x << 1) | yh))
    return pairs


def across_cores(value):
    return lax.ppermute(value, "core", [(0, 1), (1, 0)])


def time_features(timestep, freq_width):
    half_width = freq_width // 2
    freq_rates = jnp.exp(
        -math.log(10000.0) * jnp.arange(half_width, dtype=jnp.float32) / half_width
    )
    angles = timestep.astype(jnp.float32)[:, None] * freq_rates[None, :]
    return jnp.concatenate([jnp.cos(angles), jnp.sin(angles)], axis=1).astype(jnp.bfloat16)


def dot_rows(left_side, right_side):
    return lax.dot_general(
        left_side, right_side, (((1,), (1,)), ((), ())), preferred_element_type=jnp.float32
    )


def dot_plain(left_side, right_side):
    return lax.dot_general(
        left_side, right_side, (((1,), (0,)), ((), ())), preferred_element_type=jnp.float32
    )


def dot_first(left_side, right_side):
    return lax.dot_general(
        left_side, right_side, (((0,), (0,)), ((), ())), preferred_element_type=jnp.float32
    )


def two_parts(value):
    high = lax.reduce_precision(value, 8, 7)
    return high.astype(jnp.bfloat16), (value - high).astype(jnp.bfloat16)


def three_parts(value):
    high = lax.reduce_precision(value, 8, 7)
    middle = lax.reduce_precision(value - high, 8, 7)
    return [part.astype(jnp.bfloat16) for part in (high, middle, value - high - middle)]


def row_norm(x_ref):
    inputs = x_ref[...].astype(jnp.float32)
    rscale = lax.rsqrt(jnp.mean(inputs * inputs, axis=1, keepdims=True) + 1e-06)
    return rscale, inputs * rscale


def activation_kernel(
    x_ref, gain_ref, select_ref, b0, b1, w_in_ref, w_out_ref, normed_ref, hidden_ref, slope_ref
):
    rows = (b0.shape[0] // SIDE - LINES) // 2
    for n, block in enumerate((b0, b1)):
        for k in range(SIDE):
            to = pl.ds((n * SIDE + k) * rows, rows)
            w_in_ref[to, :] = block[pl.ds(2 * k * rows, rows), :]
            w_out_ref[to, :] = block[pl.ds((2 * k + 1) * rows, rows), :]
    _, unit = row_norm(x_ref)
    normed = (unit * gain_ref[...]).astype(jnp.bfloat16)
    normed_ref[...] = normed
    tail = pl.ds(2 * SIDE * rows, SIDE * LINES)
    extras = jnp.concatenate([b0[tail, :], b1[tail, :]], axis=0)
    spread = dot_plain(extras, select_ref[...])
    line = lax.broadcasted_iota(jnp.int32, spread.shape, 0)
    shard = lax.broadcasted_iota(jnp.int32, spread.shape, 1) // (rows // 2)
    mine = (line // LINES * 2 + line % LINES == shard) & (line % LINES < 2)
    cond = jnp.sum(jnp.where(mine, spread, 0.0), axis=0, keepdims=True)
    pre = dot_rows(normed, w_in_ref[...]) + cond
    sig = jax.nn.sigmoid(pre)
    hidden_ref[...] = (pre * sig).astype(jnp.bfloat16)
    slope_ref[...] = sig * (1.0 + pre * (1.0 - sig))


def turn_body(g_ref, x_ref, gain_ref, quarters):
    grad = g_ref[...]
    total = None
    pre_grads = []
    for w_in_ref, w_out_ref, slope_ref in quarters:
        pre_grad = dot_rows(grad, w_out_ref[...]) * slope_ref[...]
        pre_grads.append(pre_grad.astype(jnp.bfloat16))
        term = dot_plain(pre_grads[-1], w_in_ref[...])
        total = term if total is None else total + term
    rscale, unit = row_norm(x_ref)
    scaled = total * gain_ref[...]
    inner = jnp.mean(scaled * unit, axis=1, keepdims=True)
    grad_in = grad.astype(jnp.float32) + rscale * (scaled - unit * inner)
    return grad_in.astype(jnp.bfloat16), total * unit, pre_grads


def turn_kernel(g, x, gain, *refs):
    quarters = [refs[i : i + 3] for i in range(0, 12, 3)]
    refs[12][...] = turn_body(g, x, gain, quarters)[0]


def last_turn_kernel(g, x, gain, *refs):
    quarters = [refs[i : i + 3] for i in range(0, 12, 3)]
    normed, out, gain_out, near_0, near_1, far_out = refs[12:]
    grad_in, terms, pre_grads = turn_body(g, x, gain, quarters)
    out[...] = grad_in
    gain_out[...] = jnp.sum(terms, axis=0, keepdims=True)
    near_0[...], near_1[...] = pre_grads[:2]
    for n, pre_grad in enumerate(pre_grads[2:]):
        rows = pl.ds(n * pre_grad.shape[1], pre_grad.shape[1])
        far_out[rows, :] = dot_first(pre_grad, normed[...]).astype(jnp.bfloat16)


def outer_kernel(left_0, left_1, right, out):
    for n, left in enumerate((left_0, left_1)):
        rows = pl.ds(n * left.shape[1], left.shape[1])
        out[rows, :] = dot_first(left[...], right[...]).astype(jnp.bfloat16)


def copy_kernel(value, out):
    out[...] = value[...]


def high_low_rows(value):
    line = lax.broadcasted_iota(jnp.int32, (PAD, value.shape[1]), 0)
    high = value.astype(jnp.bfloat16).astype(jnp.float32)
    rows = jnp.where(line == 0, high, jnp.where(line == 1, value - high, 0.0))
    return rows.astype(jnp.bfloat16)


def near_kernel(
    pg_0, pg_1, normed, in_far, hidden_0, hidden_1, grad, out_far, gain_here, gain_there, *sums
):
    rows = (sums[0].shape[0] - PAD) // SIDE // 2
    products = (((pg_0, pg_1), normed, in_far), ((hidden_0, hidden_1), grad, out_far))
    for first, (lefts, right, far) in enumerate(products):
        for n, left in enumerate(lefts):
            width = left.shape[1]
            total = dot_first(left[...], right[...])
            total = total + far[pl.ds(n * width, width), :].astype(jnp.float32)
            total = total.astype(jnp.bfloat16)
            for k in range(width // rows):
                peer = n * width // rows + k
                to = pl.ds((peer % SIDE * 2 + first) * rows, rows)
                sums[peer // SIDE][to, :] = total[k * rows : (k + 1) * rows, :]
    gain = high_low_rows(gain_here[...] + gain_there[...])
    for out in sums:
        out[pl.ds(out.shape[0] - PAD, PAD), :] = gain


def stage_sum_kernel(s0, s1, s2, s3, *outs):
    rows = outs[0].shape[0] - PAD
    for k, out in enumerate(outs):
        cut = pl.ds(k * rows, rows)
        total = sum(s[cut, :].astype(jnp.float32) for s in (s0, s1, s2, s3))
        out[pl.ds(0, rows), :] = total.astype(jnp.bfloat16)
    tail = pl.ds(s0.shape[0] - PAD, PAD)
    total = sum(s[tail, :].astype(jnp.float32) for s in (s0, s1, s2, s3))
    gain = high_low_rows(jnp.sum(total, axis=0, keepdims=True))
    for out in outs:
        out[pl.ds(rows, PAD), :] = gain


def kernel(body, outs, flops=0):
    whole = pl.BlockSpec(memory_space=pltpu.VMEM)
    shapes = [jax.ShapeDtypeStruct(*out) for out in outs]

    def call(*operands):
        result = pl.pallas_call(
            body,
            out_shape=shapes,
            in_specs=[whole] * len(operands),
            out_specs=[whole] * len(shapes),
            compiler_params=pltpu.CompilerParams(vmem_limit_bytes=VMEM_LIMIT),
            cost_estimate=pl.CostEstimate(flops=flops, bytes_accessed=4 << 20, transcendentals=0),
        )(*operands)
        return result if len(shapes) > 1 else result[0]

    return call


def on_device(checkpoints, cotangent, gains, w_in, w_out, time_proj, class_table, timestep, label):
    rows, chan = checkpoints.shape[1:]
    own = w_in.shape[2]
    half = SIDE * SIDE * 2 * own
    grad_scale = float(rows * 64) ** (-0.5)
    section = lax.axis_index("z") % 4
    sample = 2 * lax.axis_index("x") + lax.axis_index("z") // 4
    bf16, f32 = jnp.bfloat16, jnp.float32

    time_feats = time_features(timestep, time_proj.shape[1])
    picks = (
        label[:, None] == jnp.arange(class_table.shape[1], dtype=jnp.int32)[None, :]
    ).astype(bf16)
    cond = dot_plain(time_feats, time_proj[0]) + dot_plain(picks, class_table[0])
    cond_row = jnp.concatenate([part.reshape(1, -1) for part in two_parts(cond)], axis=1)
    shard = jnp.concatenate(
        [w_in[0].T, w_out[0], cond_row, jnp.zeros((7, chan), bf16)], axis=0
    )

    one, two = (lax.ppermute(shard, COLUMN, home_to_work(flip)) for flip in (0, 1))
    packed = jnp.concatenate(
        [checkpoints[0], cotangent, *three_parts(gains), jnp.zeros((PAD - 3, chan), bf16)], axis=0
    )
    packed = lax.ppermute(packed, COLUMN, home_to_work(0))
    x_rows, cot_rows = packed[:rows], packed[rows : 2 * rows]
    gain_row = packed[2 * rows : 2 * rows + 3].astype(f32)
    gain_row = gain_row[0:1] + gain_row[1:2] + gain_row[2:3]

    chunk = jnp.concatenate(
        [
            one[:own],
            two[:own],
            one[own : 2 * own],
            two[own : 2 * own],
            one[2 * own : 2 * own + 1],
            two[2 * own : 2 * own + 1],
            jnp.zeros((LINES - 2, chan), bf16),
        ],
        axis=0,
    )
    chunks = [chunk] + [lax.ppermute(chunk, PLANE, along(1, k)) for k in range(1, SIDE)]
    quarter = jnp.concatenate(
        [part[: 4 * own] for part in chunks] + [part[4 * own :] for part in chunks], axis=0
    )
    near = [quarter] + [lax.ppermute(quarter, PLANE, along(2, k)) for k in range(1, SIDE)]

    width = half // 2
    entry = jnp.arange(chan, dtype=jnp.int32)[:, None]
    hidden_col = jnp.arange(width, dtype=jnp.int32)[None, :]
    select = (
        (entry % own == hidden_col % own) & (entry // own % SAMPLES == sample)
    ).astype(bf16)

    flops = 2 * rows * half * chan
    activate = kernel(
        activation_kernel,
        [
            ((width, chan), bf16),
            ((width, chan), bf16),
            ((rows, chan), bf16),
            ((rows, width), bf16),
            ((rows, width), f32),
        ],
        flops,
    )
    first_far = [across_cores(block) for block in near[:2]]
    first = [activate(x_rows, gain_row, select, *blocks) for blocks in (near[:2], first_far)]
    last_near, *first = lax.optimization_barrier((near[3], *first))
    near, last_far = [near[2], last_near], [across_cores(near[2]), across_cores(last_near)]
    second = [activate(x_rows, gain_row, select, *blocks) for blocks in (near, last_far)]
    quarters = [first[0], second[0], first[1], second[1]]
    normed = quarters[0][2]
    hiddens = [quarter[3] for quarter in quarters]
    held = [x_rows, gain_row]
    for w_in_rows, w_out_rows, _, _, slope in quarters:
        held += [w_in_rows, w_out_rows, slope]

    turn = kernel(turn_kernel, [((rows, chan), bf16)], 4 * flops)
    grad = jnp.where(section == 3, cot_rows, jnp.zeros_like(cot_rows))
    kept = grad
    for _ in range(3):
        grad = lax.ppermute(turn(grad, *held), "z", next_section())
        kept = kept + grad

    far_out = kernel(outer_kernel, [((half, chan), bf16)], flops)(*hiddens[2:], kept)
    recv_out = across_cores(far_out)
    last_turn = kernel(
        last_turn_kernel,
        [
            ((rows, chan), bf16),
            ((1, chan), f32),
            ((rows, width), bf16),
            ((rows, width), bf16),
            ((half, chan), bf16),
        ],
        5 * flops,
    )
    grad_in, gain_part, pg_0, pg_1, far_in = last_turn(kept, *held, normed)
    recv_in = across_cores(far_in)
    gain_there = across_cores(gain_part)
    sums = kernel(near_kernel, [((SIDE * 4 * own + PAD, chan), bf16)] * SIDE, 2 * flops)(
        pg_0, pg_1, normed, recv_in, *hiddens[:2], kept, recv_out, gain_part, gain_there
    )
    grad_home = lax.ppermute(grad_in, COLUMN, work_to_home(0))
    grad_home = kernel(copy_kernel, [((rows, chan), bf16)])(grad_home)

    parts = [sums[0]] + [
        lax.ppermute(sums[k], PLANE, along(2, SIDE - k)) for k in range(1, SIDE)
    ]
    sums = kernel(stage_sum_kernel, [((4 * own + PAD, chan), bf16)] * SIDE)(*parts)
    parts = [sums[0]] + [
        lax.ppermute(sums[k], PLANE, along(1, SIDE - k)) for k in range(1, SIDE)
    ]
    total = sum(part.astype(f32) for part in parts)
    total, grad_home = lax.optimization_barrier((total, grad_home))
    gain_lines = list(two_parts(total[4 * own : 4 * own + 1] + total[4 * own + 1 : 4 * own + 2]))
    gain_lines.append(jnp.zeros((6, chan), bf16))
    total = total.astype(bf16)
    home = sum(
        lax.ppermute(
            jnp.concatenate(
                [
                    total[flip * own : (flip + 1) * own],
                    total[(2 + flip) * own : (3 + flip) * own],
                    *gain_lines,
                ],
                axis=0,
            ),
            COLUMN,
            work_to_home(flip),
        ).astype(f32)
        for flip in (0, 1)
    )
    return (
        grad_home[None],
        (home[:own].T * grad_scale)[None],
        (home[own : 2 * own] * grad_scale)[None],
        (home[2 * own : 2 * own + 1] + home[2 * own + 1 : 2 * own + 2]) * grad_scale,
    )


def solution(mesh):
    fine = Mesh(mesh.devices.reshape(2, 2, 4, 8, 2), ALL)
    section, fsdp = ("yl", "core"), ("x", "z", "yh")
    in_specs = (
        P(section, fsdp, None),
        P(fsdp, None),
        P(section, None),
        P(section, None, fsdp),
        P(section, fsdp, None),
        P(section, None, fsdp),
        P(section, None, fsdp),
        P(),
        P(),
    )
    out_specs = (
        P(section, fsdp, None),
        P(section, None, fsdp),
        P(section, fsdp, None),
        P(section, None),
    )
    return jax.shard_map(
        on_device, mesh=fine, in_specs=in_specs, out_specs=out_specs, check_vma=False
    )
```

```python
import math

import jax
import jax.numpy as jnp
from jax import lax
from jax.experimental import pallas as pl
from jax.experimental.pallas import tpu as pltpu
from jax.sharding import Mesh, PartitionSpec as P

SAMPLES = 8
COLUMN = ("yl", "core", "z", "yh")
PLANE = ("yl", "core", "x", "yh")
SIDE = 4
PAD = 16
LINES = 8
VMEM_LIMIT = 28 << 20
ALL = ("yl", "core", "x", "z", "yh")


def home_to_work(flip):
    pairs = []
    for i in range(64):
        sec, z2, z10, yh = i >> 4, (i >> 3) & 1, (i >> 1) & 3, i & 1
        pairs.append((i, (z10 << 4) | ((z2 ^ flip) << 3) | (sec << 1) | yh))
    return pairs


def work_to_home(flip):
    return [(j, i) for i, j in home_to_work(flip)]


def next_section():
    return [(z, (z - 1) % 8) for z in range(8)]


def along(stage, shift):
    pairs = []
    for i in range(32):
        yl, core, x, yh = i >> 4, (i >> 3) & 1, (i >> 1) & 3, i & 1
        if (core == 0) == (stage == 1):
            x = (x + shift) % SIDE
        else:
            y = (2 * yh + yl + shift) % SIDE
            yl, yh = y % 2, y // 2
        pairs.append((i, (yl << 4) | (core << 3) | (x << 1) | yh))
    return pairs


def across_cores(value):
    return lax.ppermute(value, "core", [(0, 1), (1, 0)])


def time_features(timestep, freq_width):
    half_width = freq_width // 2
    freq_rates = jnp.exp(
        -math.log(10000.0) * jnp.arange(half_width, dtype=jnp.float32) / half_width
    )
    angles = timestep.astype(jnp.float32)[:, None] * freq_rates[None, :]
    return jnp.concatenate([jnp.cos(angles), jnp.sin(angles)], axis=1).astype(jnp.bfloat16)


def dot_rows(left_side, right_side):
    return lax.dot_general(
        left_side, right_side, (((1,), (1,)), ((), ())), preferred_element_type=jnp.float32
    )


def dot_plain(left_side, right_side):
    return lax.dot_general(
        left_side, right_side, (((1,), (0,)), ((), ())), preferred_element_type=jnp.float32
    )


def dot_first(left_side, right_side):
    return lax.dot_general(
        left_side, right_side, (((0,), (0,)), ((), ())), preferred_element_type=jnp.float32
    )


def two_parts(value):
    high = lax.reduce_precision(value, 8, 7)
    return high.astype(jnp.bfloat16), (value - high).astype(jnp.bfloat16)


def three_parts(value):
    high = lax.reduce_precision(value, 8, 7)
    middle = lax.reduce_precision(value - high, 8, 7)
    return [part.astype(jnp.bfloat16) for part in (high, middle, value - high - middle)]


def row_norm(x_ref):
    inputs = x_ref[...].astype(jnp.float32)
    rscale = lax.rsqrt(jnp.mean(inputs * inputs, axis=1, keepdims=True) + 1e-06)
    return rscale, inputs * rscale


def activation_kernel(
    x_ref, gain_ref, select_ref, b0, b1, w_in_ref, w_out_ref, normed_ref, hidden_ref, slope_ref
):
    rows = (b0.shape[0] // SIDE - LINES) // 2
    for n, block in enumerate((b0, b1)):
        for k in range(SIDE):
            to = pl.ds((n * SIDE + k) * rows, rows)
            w_in_ref[to, :] = block[pl.ds(2 * k * rows, rows), :]
            w_out_ref[to, :] = block[pl.ds((2 * k + 1) * rows, rows), :]
    _, unit = row_norm(x_ref)
    normed = (unit * gain_ref[...]).astype(jnp.bfloat16)
    normed_ref[...] = normed
    tail = pl.ds(2 * SIDE * rows, SIDE * LINES)
    extras = jnp.concatenate([b0[tail, :], b1[tail, :]], axis=0)
    spread = dot_plain(extras, select_ref[...])
    line = lax.broadcasted_iota(jnp.int32, spread.shape, 0)
    shard = lax.broadcasted_iota(jnp.int32, spread.shape, 1) // (rows // 2)
    mine = (line // LINES * 2 + line % LINES == shard) & (line % LINES < 2)
    cond = jnp.sum(jnp.where(mine, spread, 0.0), axis=0, keepdims=True)
    pre = dot_rows(normed, w_in_ref[...]) + cond
    sig = jax.nn.sigmoid(pre)
    hidden_ref[...] = (pre * sig).astype(jnp.bfloat16)
    slope_ref[...] = sig * (1.0 + pre * (1.0 - sig))


def turn_body(g_ref, x_ref, gain_ref, quarters):
    grad = g_ref[...]
    total = None
    pre_grads = []
    for w_in_ref, w_out_ref, slope_ref in quarters:
        pre_grad = dot_rows(grad, w_out_ref[...]) * slope_ref[...]
        pre_grads.append(pre_grad.astype(jnp.bfloat16))
        term = dot_plain(pre_grads[-1], w_in_ref[...])
        total = term if total is None else total + term
    rscale, unit = row_norm(x_ref)
    scaled = total * gain_ref[...]
    inner = jnp.mean(scaled * unit, axis=1, keepdims=True)
    grad_in = grad.astype(jnp.float32) + rscale * (scaled - unit * inner)
    return grad_in.astype(jnp.bfloat16), total * unit, pre_grads


def turn_kernel(g, x, gain, *refs):
    quarters = [refs[i : i + 3] for i in range(0, 12, 3)]
    refs[12][...] = turn_body(g, x, gain, quarters)[0]


def last_turn_kernel(g, x, gain, *refs):
    quarters = [refs[i : i + 3] for i in range(0, 12, 3)]
    out, gain_out = refs[12:14]
    grad_in, terms, pre_grads = turn_body(g, x, gain, quarters)
    out[...] = grad_in
    gain_out[...] = jnp.sum(terms, axis=0, keepdims=True)
    for ref, pre_grad in zip(refs[14:], pre_grads):
        ref[...] = pre_grad


def outer_kernel(left_0, left_1, right, out):
    for n, left in enumerate((left_0, left_1)):
        rows = pl.ds(n * left.shape[1], left.shape[1])
        out[rows, :] = dot_first(left[...], right[...]).astype(jnp.bfloat16)


def copy_kernel(value, out):
    out[...] = value[...]


def high_low_rows(value):
    line = lax.broadcasted_iota(jnp.int32, (PAD, value.shape[1]), 0)
    high = value.astype(jnp.bfloat16).astype(jnp.float32)
    rows = jnp.where(line == 0, high, jnp.where(line == 1, value - high, 0.0))
    return rows.astype(jnp.bfloat16)


def near_kernel(
    pg_0, pg_1, normed, in_far, hidden_0, hidden_1, grad, out_far, gain_here, gain_there, *sums
):
    rows = (sums[0].shape[0] - PAD) // SIDE // 2
    products = (((pg_0, pg_1), normed, in_far), ((hidden_0, hidden_1), grad, out_far))
    for first, (lefts, right, far) in enumerate(products):
        for n, left in enumerate(lefts):
            width = left.shape[1]
            total = dot_first(left[...], right[...])
            total = total + far[pl.ds(n * width, width), :].astype(jnp.float32)
            total = total.astype(jnp.bfloat16)
            for k in range(width // rows):
                peer = n * width // rows + k
                to = pl.ds((peer % SIDE * 2 + first) * rows, rows)
                sums[peer // SIDE][to, :] = total[k * rows : (k + 1) * rows, :]
    gain = high_low_rows(gain_here[...] + gain_there[...])
    for out in sums:
        out[pl.ds(out.shape[0] - PAD, PAD), :] = gain


def stage_sum_kernel(s0, s1, s2, s3, *outs):
    rows = outs[0].shape[0] - PAD
    for k, out in enumerate(outs):
        cut = pl.ds(k * rows, rows)
        total = sum(s[cut, :].astype(jnp.float32) for s in (s0, s1, s2, s3))
        out[pl.ds(0, rows), :] = total.astype(jnp.bfloat16)
    tail = pl.ds(s0.shape[0] - PAD, PAD)
    total = sum(s[tail, :].astype(jnp.float32) for s in (s0, s1, s2, s3))
    gain = high_low_rows(jnp.sum(total, axis=0, keepdims=True))
    for out in outs:
        out[pl.ds(rows, PAD), :] = gain


def kernel(body, outs, flops=0):
    whole = pl.BlockSpec(memory_space=pltpu.VMEM)
    shapes = [jax.ShapeDtypeStruct(*out) for out in outs]

    def call(*operands):
        result = pl.pallas_call(
            body,
            out_shape=shapes,
            in_specs=[whole] * len(operands),
            out_specs=[whole] * len(shapes),
            compiler_params=pltpu.CompilerParams(vmem_limit_bytes=VMEM_LIMIT),
            cost_estimate=pl.CostEstimate(flops=flops, bytes_accessed=4 << 20, transcendentals=0),
        )(*operands)
        return result if len(shapes) > 1 else result[0]

    return call


def on_device(checkpoints, cotangent, gains, w_in, w_out, time_proj, class_table, timestep, label):
    rows, chan = checkpoints.shape[1:]
    own = w_in.shape[2]
    half = SIDE * SIDE * 2 * own
    grad_scale = float(rows * 64) ** (-0.5)
    section = lax.axis_index("z") % 4
    sample = 2 * lax.axis_index("x") + lax.axis_index("z") // 4
    bf16, f32 = jnp.bfloat16, jnp.float32

    time_feats = time_features(timestep, time_proj.shape[1])
    picks = (
        label[:, None] == jnp.arange(class_table.shape[1], dtype=jnp.int32)[None, :]
    ).astype(bf16)
    cond = dot_plain(time_feats, time_proj[0]) + dot_plain(picks, class_table[0])
    cond_row = jnp.concatenate([part.reshape(1, -1) for part in two_parts(cond)], axis=1)
    shard = jnp.concatenate(
        [w_in[0].T, w_out[0], cond_row, jnp.zeros((7, chan), bf16)], axis=0
    )

    one, two = (lax.ppermute(shard, COLUMN, home_to_work(flip)) for flip in (0, 1))
    chunk = jnp.concatenate(
        [
            one[:own],
            two[:own],
            one[own : 2 * own],
            two[own : 2 * own],
            one[2 * own : 2 * own + 1],
            two[2 * own : 2 * own + 1],
            jnp.zeros((LINES - 2, chan), bf16),
        ],
        axis=0,
    )
    chunks = [chunk] + [lax.ppermute(chunk, PLANE, along(1, k)) for k in range(1, SIDE)]
    quarter = jnp.concatenate(
        [part[: 4 * own] for part in chunks] + [part[4 * own :] for part in chunks], axis=0
    )
    packed = jnp.concatenate(
        [checkpoints[0], cotangent, *three_parts(gains), jnp.zeros((PAD - 3, chan), bf16)], axis=0
    )
    packed = lax.ppermute(packed, COLUMN, home_to_work(0))
    quarter, packed = lax.optimization_barrier((quarter, packed))
    x_rows, cot_rows = packed[:rows], packed[rows : 2 * rows]
    gain_row = packed[2 * rows : 2 * rows + 3].astype(f32)
    gain_row = gain_row[0:1] + gain_row[1:2] + gain_row[2:3]
    near = [quarter] + [lax.ppermute(quarter, PLANE, along(2, k)) for k in range(1, SIDE)]

    width = half // 2
    entry = jnp.arange(chan, dtype=jnp.int32)[:, None]
    hidden_col = jnp.arange(width, dtype=jnp.int32)[None, :]
    select = (
        (entry % own == hidden_col % own) & (entry // own % SAMPLES == sample)
    ).astype(bf16)

    flops = 2 * rows * half * chan
    activate = kernel(
        activation_kernel,
        [
            ((width, chan), bf16),
            ((width, chan), bf16),
            ((rows, chan), bf16),
            ((rows, width), bf16),
            ((rows, width), f32),
        ],
        flops,
    )
    first_far = [across_cores(block) for block in near[:2]]
    first = [activate(x_rows, gain_row, select, *blocks) for blocks in (near[:2], first_far)]
    last_near, *first = lax.optimization_barrier((near[3], *first))
    near, last_far = [near[2], last_near], [across_cores(near[2]), across_cores(last_near)]
    second = [activate(x_rows, gain_row, select, *blocks) for blocks in (near, last_far)]
    quarters = [first[0], second[0], first[1], second[1]]
    normed = quarters[0][2]
    hiddens = [quarter[3] for quarter in quarters]
    held = [x_rows, gain_row]
    for w_in_rows, w_out_rows, _, _, slope in quarters:
        held += [w_in_rows, w_out_rows, slope]

    turn = kernel(turn_kernel, [((rows, chan), bf16)], 4 * flops)
    grad = jnp.where(section == 3, cot_rows, jnp.zeros_like(cot_rows))
    kept = grad
    for _ in range(3):
        grad = lax.ppermute(turn(grad, *held), "z", next_section())
        kept = kept + grad

    outer = kernel(outer_kernel, [((half, chan), bf16)], flops)
    far_out = outer(*hiddens[2:], kept)
    kept, far_out = lax.optimization_barrier((kept, far_out))
    recv_out = across_cores(far_out)
    last_turn = kernel(
        last_turn_kernel,
        [((rows, chan), bf16), ((1, chan), f32)] + [((rows, width), bf16)] * 4,
        4 * flops,
    )
    grad_in, gain_part, pg_0, pg_1, *pg_far = last_turn(kept, *held)
    *pg_far, recv_out = lax.optimization_barrier((*pg_far, recv_out))
    recv_in = across_cores(outer(*pg_far, normed))
    gain_there = across_cores(gain_part)
    sums = kernel(near_kernel, [((SIDE * 4 * own + PAD, chan), bf16)] * SIDE, 2 * flops)(
        pg_0, pg_1, normed, recv_in, *hiddens[:2], kept, recv_out, gain_part, gain_there
    )
    grad_home = lax.ppermute(grad_in, COLUMN, work_to_home(0))
    grad_home = kernel(copy_kernel, [((rows, chan), bf16)])(grad_home)

    parts = [sums[0]] + [
        lax.ppermute(sums[k], PLANE, along(2, SIDE - k)) for k in range(1, SIDE)
    ]
    *parts, grad_home = lax.optimization_barrier((*parts, grad_home))
    sums = kernel(stage_sum_kernel, [((4 * own + PAD, chan), bf16)] * SIDE)(*parts)
    parts = [sums[0]] + [
        lax.ppermute(sums[k], PLANE, along(1, SIDE - k)) for k in range(1, SIDE)
    ]
    total = sum(part.astype(f32) for part in parts)
    gain_lines = list(two_parts(total[4 * own : 4 * own + 1] + total[4 * own + 1 : 4 * own + 2]))
    gain_lines.append(jnp.zeros((6, chan), bf16))
    total = total.astype(bf16)
    home = sum(
        lax.ppermute(
            jnp.concatenate(
                [
                    total[flip * own : (flip + 1) * own],
                    total[(2 + flip) * own : (3 + flip) * own],
                    *gain_lines,
                ],
                axis=0,
            ),
            COLUMN,
            work_to_home(flip),
        ).astype(f32)
        for flip in (0, 1)
    )
    return (
        grad_home[None],
        (home[:own].T * grad_scale)[None],
        (home[own : 2 * own] * grad_scale)[None],
        (home[2 * own : 2 * own + 1] + home[2 * own + 1 : 2 * own + 2]) * grad_scale,
    )


def solution(mesh):
    fine = Mesh(mesh.devices.reshape(2, 2, 4, 8, 2), ALL)
    section, fsdp = ("yl", "core"), ("x", "z", "yh")
    in_specs = (
        P(section, fsdp, None),
        P(fsdp, None),
        P(section, None),
        P(section, None, fsdp),
        P(section, fsdp, None),
        P(section, None, fsdp),
        P(section, None, fsdp),
        P(),
        P(),
    )
    out_specs = (
        P(section, fsdp, None),
        P(section, None, fsdp),
        P(section, fsdp, None),
        P(section, None),
    )
    return jax.shard_map(
        on_device, mesh=fine, in_specs=in_specs, out_specs=out_specs, check_vma=False
    )
```

```python
import math

import jax
import jax.numpy as jnp
from jax import lax
from jax.experimental import pallas as pl
from jax.experimental.pallas import tpu as pltpu
from jax.sharding import Mesh, PartitionSpec as P

SAMPLES = 8
COLUMN = ("yl", "core", "z", "yh")
PLANE = ("yl", "core", "x", "yh")
SIDE = 4
PAD = 16
LINES = 8
VMEM_LIMIT = 28 << 20
ALL = ("yl", "core", "x", "z", "yh")


def home_to_work(flip):
    pairs = []
    for i in range(64):
        sec, z2, z10, yh = i >> 4, (i >> 3) & 1, (i >> 1) & 3, i & 1
        pairs.append((i, (z10 << 4) | ((z2 ^ flip) << 3) | (sec << 1) | yh))
    return pairs


def work_to_home(flip):
    return [(j, i) for i, j in home_to_work(flip)]


def next_section():
    return [(z, (z - 1) % 8) for z in range(8)]


def along(stage, shift):
    pairs = []
    for i in range(32):
        yl, core, x, yh = i >> 4, (i >> 3) & 1, (i >> 1) & 3, i & 1
        if (core == 0) == (stage == 1):
            x = (x + shift) % SIDE
        else:
            y = (2 * yh + yl + shift) % SIDE
            yl, yh = y % 2, y // 2
        pairs.append((i, (yl << 4) | (core << 3) | (x << 1) | yh))
    return pairs


def across_cores(value):
    return lax.ppermute(value, "core", [(0, 1), (1, 0)])


def time_features(timestep, freq_width):
    half_width = freq_width // 2
    freq_rates = jnp.exp(
        -math.log(10000.0) * jnp.arange(half_width, dtype=jnp.float32) / half_width
    )
    angles = timestep.astype(jnp.float32)[:, None] * freq_rates[None, :]
    return jnp.concatenate([jnp.cos(angles), jnp.sin(angles)], axis=1).astype(jnp.bfloat16)


def dot_rows(left_side, right_side):
    return lax.dot_general(
        left_side, right_side, (((1,), (1,)), ((), ())), preferred_element_type=jnp.float32
    )


def dot_plain(left_side, right_side):
    return lax.dot_general(
        left_side, right_side, (((1,), (0,)), ((), ())), preferred_element_type=jnp.float32
    )


def dot_first(left_side, right_side):
    return lax.dot_general(
        left_side, right_side, (((0,), (0,)), ((), ())), preferred_element_type=jnp.float32
    )


def two_parts(value):
    high = lax.reduce_precision(value, 8, 7)
    return high.astype(jnp.bfloat16), (value - high).astype(jnp.bfloat16)


def three_parts(value):
    high = lax.reduce_precision(value, 8, 7)
    middle = lax.reduce_precision(value - high, 8, 7)
    return [part.astype(jnp.bfloat16) for part in (high, middle, value - high - middle)]


def row_norm(x_ref):
    inputs = x_ref[...].astype(jnp.float32)
    rscale = lax.rsqrt(jnp.mean(inputs * inputs, axis=1, keepdims=True) + 1e-06)
    return rscale, inputs * rscale


def activation_kernel(
    x_ref, gain_ref, select_ref, b0, b1, w_in_ref, w_out_ref, normed_ref, hidden_ref, slope_ref
):
    rows = (b0.shape[0] // SIDE - LINES) // 2
    for n, block in enumerate((b0, b1)):
        for k in range(SIDE):
            to = pl.ds((n * SIDE + k) * rows, rows)
            w_in_ref[to, :] = block[pl.ds(2 * k * rows, rows), :]
            w_out_ref[to, :] = block[pl.ds((2 * k + 1) * rows, rows), :]
    _, unit = row_norm(x_ref)
    normed = (unit * gain_ref[...]).astype(jnp.bfloat16)
    normed_ref[...] = normed
    tail = pl.ds(2 * SIDE * rows, SIDE * LINES)
    extras = jnp.concatenate([b0[tail, :], b1[tail, :]], axis=0)
    spread = dot_plain(extras, select_ref[...])
    line = lax.broadcasted_iota(jnp.int32, spread.shape, 0)
    shard = lax.broadcasted_iota(jnp.int32, spread.shape, 1) // (rows // 2)
    mine = (line // LINES * 2 + line % LINES == shard) & (line % LINES < 2)
    cond = jnp.sum(jnp.where(mine, spread, 0.0), axis=0, keepdims=True)
    pre = dot_rows(normed, w_in_ref[...]) + cond
    sig = jax.nn.sigmoid(pre)
    hidden_ref[...] = (pre * sig).astype(jnp.bfloat16)
    slope_ref[...] = sig * (1.0 + pre * (1.0 - sig))


def turn_body(g_ref, x_ref, gain_ref, quarters):
    grad = g_ref[...]
    total = None
    pre_grads = []
    for w_in_ref, w_out_ref, slope_ref in quarters:
        pre_grad = dot_rows(grad, w_out_ref[...]) * slope_ref[...]
        pre_grads.append(pre_grad.astype(jnp.bfloat16))
        term = dot_plain(pre_grads[-1], w_in_ref[...])
        total = term if total is None else total + term
    rscale, unit = row_norm(x_ref)
    scaled = total * gain_ref[...]
    inner = jnp.mean(scaled * unit, axis=1, keepdims=True)
    grad_in = grad.astype(jnp.float32) + rscale * (scaled - unit * inner)
    return grad_in.astype(jnp.bfloat16), total * unit, pre_grads


def turn_kernel(g, x, gain, *refs):
    quarters = [refs[i : i + 3] for i in range(0, 12, 3)]
    refs[12][...] = turn_body(g, x, gain, quarters)[0]


def last_turn_kernel(g, x, gain, *refs):
    quarters = [refs[i : i + 3] for i in range(0, 12, 3)]
    out, gain_out = refs[12:14]
    grad_in, terms, pre_grads = turn_body(g, x, gain, quarters)
    out[...] = grad_in
    gain_out[...] = jnp.sum(terms, axis=0, keepdims=True)
    for ref, pre_grad in zip(refs[14:], pre_grads):
        ref[...] = pre_grad


def outer_kernel(left_0, left_1, right, out):
    for n, left in enumerate((left_0, left_1)):
        rows = pl.ds(n * left.shape[1], left.shape[1])
        out[rows, :] = dot_first(left[...], right[...]).astype(jnp.bfloat16)


def copy_kernel(value, out):
    out[...] = value[...]


def high_low_rows(value):
    line = lax.broadcasted_iota(jnp.int32, (PAD, value.shape[1]), 0)
    high = value.astype(jnp.bfloat16).astype(jnp.float32)
    rows = jnp.where(line == 0, high, jnp.where(line == 1, value - high, 0.0))
    return rows.astype(jnp.bfloat16)


def near_kernel(
    pg_0, pg_1, normed, in_far, hidden_0, hidden_1, grad, out_far, gain_here, gain_there, *sums
):
    rows = (sums[0].shape[0] - PAD) // SIDE // 2
    products = (((pg_0, pg_1), normed, in_far), ((hidden_0, hidden_1), grad, out_far))
    for first, (lefts, right, far) in enumerate(products):
        for n, left in enumerate(lefts):
            width = left.shape[1]
            total = dot_first(left[...], right[...])
            total = total + far[pl.ds(n * width, width), :].astype(jnp.float32)
            total = total.astype(jnp.bfloat16)
            for k in range(width // rows):
                peer = n * width // rows + k
                to = pl.ds((peer % SIDE * 2 + first) * rows, rows)
                sums[peer // SIDE][to, :] = total[k * rows : (k + 1) * rows, :]
    gain = high_low_rows(gain_here[...] + gain_there[...])
    for out in sums:
        out[pl.ds(out.shape[0] - PAD, PAD), :] = gain


def stage_sum_kernel(s0, s1, s2, s3, *outs):
    rows = outs[0].shape[0] - PAD
    for k, out in enumerate(outs):
        cut = pl.ds(k * rows, rows)
        total = sum(s[cut, :].astype(jnp.float32) for s in (s0, s1, s2, s3))
        out[pl.ds(0, rows), :] = total.astype(jnp.bfloat16)
    tail = pl.ds(s0.shape[0] - PAD, PAD)
    total = sum(s[tail, :].astype(jnp.float32) for s in (s0, s1, s2, s3))
    gain = high_low_rows(jnp.sum(total, axis=0, keepdims=True))
    for out in outs:
        out[pl.ds(rows, PAD), :] = gain


def kernel(body, outs, flops=0):
    whole = pl.BlockSpec(memory_space=pltpu.VMEM)
    shapes = [jax.ShapeDtypeStruct(*out) for out in outs]

    def call(*operands):
        result = pl.pallas_call(
            body,
            out_shape=shapes,
            in_specs=[whole] * len(operands),
            out_specs=[whole] * len(shapes),
            compiler_params=pltpu.CompilerParams(vmem_limit_bytes=VMEM_LIMIT),
            cost_estimate=pl.CostEstimate(flops=flops, bytes_accessed=4 << 20, transcendentals=0),
        )(*operands)
        return result if len(shapes) > 1 else result[0]

    return call


def on_device(checkpoints, cotangent, gains, w_in, w_out, time_proj, class_table, timestep, label):
    rows, chan = checkpoints.shape[1:]
    own = w_in.shape[2]
    half = SIDE * SIDE * 2 * own
    grad_scale = float(rows * 64) ** (-0.5)
    sample = 2 * lax.axis_index("x") + lax.axis_index("z") // 4
    bf16, f32 = jnp.bfloat16, jnp.float32

    time_feats = time_features(timestep, time_proj.shape[1])
    picks = (
        label[:, None] == jnp.arange(class_table.shape[1], dtype=jnp.int32)[None, :]
    ).astype(bf16)
    cond = dot_plain(time_feats, time_proj[0]) + dot_plain(picks, class_table[0])
    cond_row = jnp.concatenate([part.reshape(1, -1) for part in two_parts(cond)], axis=1)
    shard = jnp.concatenate(
        [w_in[0].T, w_out[0], cond_row, *three_parts(gains), jnp.zeros((4, chan), bf16)], axis=0
    )

    one, two = (lax.ppermute(shard, COLUMN, home_to_work(flip)) for flip in (0, 1))
    chunk = jnp.concatenate(
        [
            one[:own],
            two[:own],
            one[own : 2 * own],
            two[own : 2 * own],
            one[2 * own : 2 * own + 1],
            two[2 * own : 2 * own + 1],
            jnp.zeros((LINES - 2, chan), bf16),
        ],
        axis=0,
    )
    chunks = [chunk] + [lax.ppermute(chunk, PLANE, along(1, k)) for k in range(1, SIDE)]
    quarter = jnp.concatenate(
        [part[: 4 * own] for part in chunks] + [part[4 * own :] for part in chunks], axis=0
    )
    gain_row = one[2 * own + 1 : 2 * own + 4].astype(f32)
    gain_row = gain_row[0:1] + gain_row[1:2] + gain_row[2:3]
    x_rows = lax.ppermute(checkpoints[0], COLUMN, home_to_work(0))
    cot_rows = lax.ppermute(
        cotangent, COLUMN, [pair for pair in home_to_work(0) if pair[0] >> 4 == 3]
    )
    near = [quarter] + [lax.ppermute(quarter, PLANE, along(2, k)) for k in range(1, SIDE)]

    width = half // 2
    entry = jnp.arange(chan, dtype=jnp.int32)[:, None]
    hidden_col = jnp.arange(width, dtype=jnp.int32)[None, :]
    select = (
        (entry % own == hidden_col % own) & (entry // own % SAMPLES == sample)
    ).astype(bf16)

    flops = 2 * rows * half * chan
    activate = kernel(
        activation_kernel,
        [
            ((width, chan), bf16),
            ((width, chan), bf16),
            ((rows, chan), bf16),
            ((rows, width), bf16),
            ((rows, width), f32),
        ],
        flops,
    )
    first_far = [across_cores(block) for block in near[:2]]
    first = [activate(x_rows, gain_row, select, *blocks) for blocks in (near[:2], first_far)]
    last_near, cot_rows, *first = lax.optimization_barrier((near[3], cot_rows, *first))
    near, last_far = [near[2], last_near], [across_cores(near[2]), across_cores(last_near)]
    second = [activate(x_rows, gain_row, select, *blocks) for blocks in (near, last_far)]
    quarters = [first[0], second[0], first[1], second[1]]
    normed = quarters[0][2]
    hiddens = [quarter[3] for quarter in quarters]
    held = [x_rows, gain_row]
    for w_in_rows, w_out_rows, _, _, slope in quarters:
        held += [w_in_rows, w_out_rows, slope]

    turn = kernel(turn_kernel, [((rows, chan), bf16)], 4 * flops)
    kept = grad = cot_rows
    for _ in range(3):
        grad = lax.ppermute(turn(grad, *held), "z", next_section())
        kept = kept + grad

    outer = kernel(outer_kernel, [((half, chan), bf16)], flops)
    far_out = outer(*hiddens[2:], kept)
    kept, far_out = lax.optimization_barrier((kept, far_out))
    recv_out = across_cores(far_out)
    last_turn = kernel(
        last_turn_kernel,
        [((rows, chan), bf16), ((1, chan), f32)] + [((rows, width), bf16)] * 4,
        4 * flops,
    )
    grad_in, gain_part, pg_0, pg_1, *pg_far = last_turn(kept, *held)
    *pg_far, recv_out = lax.optimization_barrier((*pg_far, recv_out))
    recv_in = across_cores(outer(*pg_far, normed))
    gain_there = across_cores(gain_part)
    sums = kernel(near_kernel, [((SIDE * 4 * own + PAD, chan), bf16)] * SIDE, 2 * flops)(
        pg_0, pg_1, normed, recv_in, *hiddens[:2], kept, recv_out, gain_part, gain_there
    )
    grad_home = lax.ppermute(grad_in, COLUMN, work_to_home(0))
    grad_home = kernel(copy_kernel, [((rows, chan), bf16)])(grad_home)

    parts = [sums[0]] + [
        lax.ppermute(sums[k], PLANE, along(2, SIDE - k)) for k in range(1, SIDE)
    ]
    *parts, grad_home = lax.optimization_barrier((*parts, grad_home))
    sums = kernel(stage_sum_kernel, [((4 * own + PAD, chan), bf16)] * SIDE)(*parts)
    parts = [sums[0]] + [
        lax.ppermute(sums[k], PLANE, along(1, SIDE - k)) for k in range(1, SIDE)
    ]
    total = sum(part.astype(f32) for part in parts)
    gain_lines = list(two_parts(total[4 * own : 4 * own + 1] + total[4 * own + 1 : 4 * own + 2]))
    gain_lines.append(jnp.zeros((6, chan), bf16))
    total = total.astype(bf16)
    home = sum(
        lax.ppermute(
            jnp.concatenate(
                [
                    total[flip * own : (flip + 1) * own],
                    total[(2 + flip) * own : (3 + flip) * own],
                    *gain_lines,
                ],
                axis=0,
            ),
            COLUMN,
            work_to_home(flip),
        ).astype(f32)
        for flip in (0, 1)
    )
    return (
        grad_home[None],
        (home[:own].T * grad_scale)[None],
        (home[own : 2 * own] * grad_scale)[None],
        (home[2 * own : 2 * own + 1] + home[2 * own + 1 : 2 * own + 2]) * grad_scale,
    )


def solution(mesh):
    fine = Mesh(mesh.devices.reshape(2, 2, 4, 8, 2), ALL)
    section, fsdp = ("yl", "core"), ("x", "z", "yh")
    in_specs = (
        P(section, fsdp, None),
        P(fsdp, None),
        P(section, None),
        P(section, None, fsdp),
        P(section, fsdp, None),
        P(section, None, fsdp),
        P(section, None, fsdp),
        P(),
        P(),
    )
    out_specs = (
        P(section, fsdp, None),
        P(section, None, fsdp),
        P(section, fsdp, None),
        P(section, None),
    )
    return jax.shard_map(
        on_device, mesh=fine, in_specs=in_specs, out_specs=out_specs, check_vma=False
    )
```

```python
import math

import jax
import jax.numpy as jnp
from jax import lax
from jax.experimental import pallas as pl
from jax.experimental.pallas import tpu as pltpu
from jax.sharding import Mesh, PartitionSpec as P

SAMPLES = 8
COLUMN = ("yl", "core", "z", "yh")
PLANE = ("yl", "core", "x", "yh")
SIDE = 4
ORDER = (2, 1, 3)
PAD = 16
LINES = 8
VMEM_LIMIT = 28 << 20
ALL = ("yl", "core", "x", "z", "yh")


def home_to_work(flip):
    pairs = []
    for i in range(64):
        sec, z2, z10, yh = i >> 4, (i >> 3) & 1, (i >> 1) & 3, i & 1
        pairs.append((i, (z10 << 4) | ((z2 ^ flip) << 3) | (sec << 1) | yh))
    return pairs


def work_to_home(flip):
    return [(j, i) for i, j in home_to_work(flip)]


def next_section():
    return [(z, (z - 1) % 8) for z in range(8)]


def along(stage, shift):
    pairs = []
    for i in range(32):
        yl, core, x, yh = i >> 4, (i >> 3) & 1, (i >> 1) & 3, i & 1
        if (core == 0) == (stage == 1):
            x = (x + shift) % SIDE
        else:
            y = (2 * yh + yl + shift) % SIDE
            yl, yh = y % 2, y // 2
        pairs.append((i, (yl << 4) | (core << 3) | (x << 1) | yh))
    return pairs


def across_cores(value):
    return lax.ppermute(value, "core", [(0, 1), (1, 0)])


def time_features(timestep, freq_width):
    half_width = freq_width // 2
    freq_rates = jnp.exp(
        -math.log(10000.0) * jnp.arange(half_width, dtype=jnp.float32) / half_width
    )
    angles = timestep.astype(jnp.float32)[:, None] * freq_rates[None, :]
    return jnp.concatenate([jnp.cos(angles), jnp.sin(angles)], axis=1).astype(jnp.bfloat16)


def dot_rows(left_side, right_side):
    return lax.dot_general(
        left_side, right_side, (((1,), (1,)), ((), ())), preferred_element_type=jnp.float32
    )


def dot_plain(left_side, right_side):
    return lax.dot_general(
        left_side, right_side, (((1,), (0,)), ((), ())), preferred_element_type=jnp.float32
    )


def dot_first(left_side, right_side):
    return lax.dot_general(
        left_side, right_side, (((0,), (0,)), ((), ())), preferred_element_type=jnp.float32
    )


def two_parts(value):
    high = lax.reduce_precision(value, 8, 7)
    return high.astype(jnp.bfloat16), (value - high).astype(jnp.bfloat16)


def three_parts(value):
    high = lax.reduce_precision(value, 8, 7)
    middle = lax.reduce_precision(value - high, 8, 7)
    return [part.astype(jnp.bfloat16) for part in (high, middle, value - high - middle)]


def row_norm(x_ref):
    inputs = x_ref[...].astype(jnp.float32)
    rscale = lax.rsqrt(jnp.mean(inputs * inputs, axis=1, keepdims=True) + 1e-06)
    return rscale, inputs * rscale


def activation_kernel(
    x_ref, gain_ref, select_ref, b0, b1, w_in_ref, w_out_ref, normed_ref, hidden_ref, slope_ref
):
    rows = (b0.shape[0] // SIDE - LINES) // 2
    for n, block in enumerate((b0, b1)):
        for k in range(SIDE):
            to = pl.ds((n * SIDE + k) * rows, rows)
            w_in_ref[to, :] = block[pl.ds(2 * k * rows, rows), :]
            w_out_ref[to, :] = block[pl.ds((2 * k + 1) * rows, rows), :]
    _, unit = row_norm(x_ref)
    normed = (unit * gain_ref[...]).astype(jnp.bfloat16)
    normed_ref[...] = normed
    tail = pl.ds(2 * SIDE * rows, SIDE * LINES)
    extras = jnp.concatenate([b0[tail, :], b1[tail, :]], axis=0)
    spread = dot_plain(extras, select_ref[...])
    line = lax.broadcasted_iota(jnp.int32, spread.shape, 0)
    shard = lax.broadcasted_iota(jnp.int32, spread.shape, 1) // (rows // 2)
    mine = (line // LINES * 2 + line % LINES == shard) & (line % LINES < 2)
    cond = jnp.sum(jnp.where(mine, spread, 0.0), axis=0, keepdims=True)
    pre = dot_rows(normed, w_in_ref[...]) + cond
    sig = jax.nn.sigmoid(pre)
    hidden_ref[...] = (pre * sig).astype(jnp.bfloat16)
    slope_ref[...] = sig * (1.0 + pre * (1.0 - sig))


def turn_body(g_ref, x_ref, gain_ref, quarters):
    grad = g_ref[...]
    total = None
    pre_grads = []
    for w_in_ref, w_out_ref, slope_ref in quarters:
        pre_grad = dot_rows(grad, w_out_ref[...]) * slope_ref[...]
        pre_grads.append(pre_grad.astype(jnp.bfloat16))
        term = dot_plain(pre_grads[-1], w_in_ref[...])
        total = term if total is None else total + term
    rscale, unit = row_norm(x_ref)
    scaled = total * gain_ref[...]
    inner = jnp.mean(scaled * unit, axis=1, keepdims=True)
    grad_in = grad.astype(jnp.float32) + rscale * (scaled - unit * inner)
    return grad_in.astype(jnp.bfloat16), total * unit, pre_grads


def turn_kernel(g, x, gain, *refs):
    quarters = [refs[i : i + 3] for i in range(0, 12, 3)]
    refs[12][...] = turn_body(g, x, gain, quarters)[0]


def last_turn_kernel(g, x, gain, *refs):
    quarters = [refs[i : i + 3] for i in range(0, 12, 3)]
    out, gain_out = refs[12:14]
    grad_in, terms, pre_grads = turn_body(g, x, gain, quarters)
    out[...] = grad_in
    gain_out[...] = jnp.sum(terms, axis=0, keepdims=True)
    for ref, pre_grad in zip(refs[14:], pre_grads):
        ref[...] = pre_grad


def outer_kernel(left_0, left_1, right, out):
    for n, left in enumerate((left_0, left_1)):
        rows = pl.ds(n * left.shape[1], left.shape[1])
        out[rows, :] = dot_first(left[...], right[...]).astype(jnp.bfloat16)


def copy_kernel(value, out):
    out[...] = value[...]


def high_low_rows(value):
    line = lax.broadcasted_iota(jnp.int32, (PAD, value.shape[1]), 0)
    high = value.astype(jnp.bfloat16).astype(jnp.float32)
    rows = jnp.where(line == 0, high, jnp.where(line == 1, value - high, 0.0))
    return rows.astype(jnp.bfloat16)


def near_kernel(
    pg_0, pg_1, normed, in_far, hidden_0, hidden_1, grad, out_far, gain_here, gain_there, *sums
):
    rows = (sums[0].shape[0] - PAD) // SIDE // 2
    products = (((pg_0, pg_1), normed, in_far), ((hidden_0, hidden_1), grad, out_far))
    for first, (lefts, right, far) in enumerate(products):
        for n, left in enumerate(lefts):
            width = left.shape[1]
            total = dot_first(left[...], right[...])
            total = total + far[pl.ds(n * width, width), :].astype(jnp.float32)
            total = total.astype(jnp.bfloat16)
            for k in range(width // rows):
                peer = n * width // rows + k
                to = pl.ds((peer % SIDE * 2 + first) * rows, rows)
                sums[peer // SIDE][to, :] = total[k * rows : (k + 1) * rows, :]
    gain = high_low_rows(gain_here[...] + gain_there[...])
    for out in sums:
        out[pl.ds(out.shape[0] - PAD, PAD), :] = gain


def stage_sum_kernel(s0, s1, s2, s3, *outs):
    rows = outs[0].shape[0] - PAD
    for k, out in enumerate(outs):
        cut = pl.ds(k * rows, rows)
        total = sum(s[cut, :].astype(jnp.float32) for s in (s0, s1, s2, s3))
        out[pl.ds(0, rows), :] = total.astype(jnp.bfloat16)
    tail = pl.ds(s0.shape[0] - PAD, PAD)
    total = sum(s[tail, :].astype(jnp.float32) for s in (s0, s1, s2, s3))
    gain = high_low_rows(jnp.sum(total, axis=0, keepdims=True))
    for out in outs:
        out[pl.ds(rows, PAD), :] = gain


def kernel(body, outs, flops=0):
    whole = pl.BlockSpec(memory_space=pltpu.VMEM)
    shapes = [jax.ShapeDtypeStruct(*out) for out in outs]

    def call(*operands):
        result = pl.pallas_call(
            body,
            out_shape=shapes,
            in_specs=[whole] * len(operands),
            out_specs=[whole] * len(shapes),
            compiler_params=pltpu.CompilerParams(vmem_limit_bytes=VMEM_LIMIT),
            cost_estimate=pl.CostEstimate(flops=flops, bytes_accessed=4 << 20, transcendentals=0),
        )(*operands)
        return result if len(shapes) > 1 else result[0]

    return call


def on_device(checkpoints, cotangent, gains, w_in, w_out, time_proj, class_table, timestep, label):
    rows, chan = checkpoints.shape[1:]
    own = w_in.shape[2]
    half = SIDE * SIDE * 2 * own
    grad_scale = float(rows * 64) ** (-0.5)
    sample = 2 * lax.axis_index("x") + lax.axis_index("z") // 4
    bf16, f32 = jnp.bfloat16, jnp.float32

    time_feats = time_features(timestep, time_proj.shape[1])
    picks = (
        label[:, None] == jnp.arange(class_table.shape[1], dtype=jnp.int32)[None, :]
    ).astype(bf16)
    cond = dot_plain(time_feats, time_proj[0]) + dot_plain(picks, class_table[0])
    cond_row = jnp.concatenate([part.reshape(1, -1) for part in two_parts(cond)], axis=1)
    line = jnp.arange(8, dtype=jnp.int32)[:, None]
    spare = jnp.zeros((8, chan), bf16)
    for n, row in enumerate((cond_row, *three_parts(gains))):
        spare = jnp.where(line == n, row, spare)
    shard = jnp.concatenate([w_in[0].T, w_out[0], spare], axis=0)

    one, two = (lax.ppermute(shard, COLUMN, home_to_work(flip)) for flip in (0, 1))
    chunk = jnp.concatenate(
        [
            one[:own],
            two[:own],
            one[own : 2 * own],
            two[own : 2 * own],
            one[2 * own : 2 * own + 1],
            two[2 * own : 2 * own + 1],
            jnp.zeros((LINES - 2, chan), bf16),
        ],
        axis=0,
    )
    chunks = [chunk] + [lax.ppermute(chunk, PLANE, along(1, k)) for k in ORDER]
    quarter = jnp.concatenate(
        [part[: 4 * own] for part in chunks] + [part[4 * own :] for part in chunks], axis=0
    )
    gain_row = one[2 * own + 1 : 2 * own + 4].astype(f32)
    gain_row = gain_row[0:1] + gain_row[1:2] + gain_row[2:3]
    x_rows = lax.ppermute(checkpoints[0], COLUMN, home_to_work(0))
    cot_rows = lax.ppermute(
        cotangent, COLUMN, [pair for pair in home_to_work(0) if pair[0] >> 4 == 3]
    )
    near = [quarter] + [lax.ppermute(quarter, PLANE, along(2, k)) for k in ORDER]

    width = half // 2
    entry = jnp.arange(chan, dtype=jnp.int32)[:, None]
    hidden_col = jnp.arange(width, dtype=jnp.int32)[None, :]
    select = (
        (entry % own == hidden_col % own) & (entry // own % SAMPLES == sample)
    ).astype(bf16)

    flops = 2 * rows * half * chan
    activate = kernel(
        activation_kernel,
        [
            ((width, chan), bf16),
            ((width, chan), bf16),
            ((rows, chan), bf16),
            ((rows, width), bf16),
            ((rows, width), f32),
        ],
        flops,
    )
    first_far = [across_cores(block) for block in near[:2]]
    first = [activate(x_rows, gain_row, select, *blocks) for blocks in (near[:2], first_far)]
    last_near, cot_rows, *first = lax.optimization_barrier((near[3], cot_rows, *first))
    near, last_far = [near[2], last_near], [across_cores(near[2]), across_cores(last_near)]
    second = [activate(x_rows, gain_row, select, *blocks) for blocks in (near, last_far)]
    quarters = [first[0], second[0], first[1], second[1]]
    normed = quarters[0][2]
    hiddens = [quarter[3] for quarter in quarters]
    held = [x_rows, gain_row]
    for w_in_rows, w_out_rows, _, _, slope in quarters:
        held += [w_in_rows, w_out_rows, slope]

    turn = kernel(turn_kernel, [((rows, chan), bf16)], 4 * flops)
    kept = grad = cot_rows
    for _ in range(3):
        grad = lax.ppermute(turn(grad, *held), "z", next_section())
        kept = kept + grad

    outer = kernel(outer_kernel, [((half, chan), bf16)], flops)
    far_out = outer(*hiddens[2:], kept)
    kept, far_out = lax.optimization_barrier((kept, far_out))
    recv_out = across_cores(far_out)
    last_turn = kernel(
        last_turn_kernel,
        [((rows, chan), bf16), ((1, chan), f32)] + [((rows, width), bf16)] * 4,
        4 * flops,
    )
    grad_in, gain_part, pg_0, pg_1, *pg_far = last_turn(kept, *held)
    *pg_far, recv_out = lax.optimization_barrier((*pg_far, recv_out))
    recv_in = across_cores(outer(*pg_far, normed))
    gain_there = across_cores(gain_part)
    sums = kernel(near_kernel, [((SIDE * 4 * own + PAD, chan), bf16)] * SIDE, 2 * flops)(
        pg_0, pg_1, normed, recv_in, *hiddens[:2], kept, recv_out, gain_part, gain_there
    )
    grad_home = lax.ppermute(grad_in, COLUMN, work_to_home(0))
    grad_home = kernel(copy_kernel, [((rows, chan), bf16)])(grad_home)

    parts = [sums[0]] + [
        lax.ppermute(part, PLANE, along(2, SIDE - k)) for k, part in zip(ORDER, sums[1:])
    ]
    *parts, grad_home = lax.optimization_barrier((*parts, grad_home))
    sums = kernel(stage_sum_kernel, [((4 * own + PAD, chan), bf16)] * SIDE)(*parts)
    parts = [sums[0]] + [
        lax.ppermute(part, PLANE, along(1, SIDE - k)) for k, part in zip(ORDER, sums[1:])
    ]
    total = sum(part.astype(f32) for part in parts)
    gain_lines = list(two_parts(total[4 * own : 4 * own + 1] + total[4 * own + 1 : 4 * own + 2]))
    gain_lines.append(jnp.zeros((6, chan), bf16))
    total = total.astype(bf16)
    home = sum(
        lax.ppermute(
            jnp.concatenate(
                [
                    total[flip * own : (flip + 1) * own],
                    total[(2 + flip) * own : (3 + flip) * own],
                    *gain_lines,
                ],
                axis=0,
            ),
            COLUMN,
            work_to_home(flip),
        ).astype(f32)
        for flip in (0, 1)
    )
    return (
        grad_home[None],
        (home[:own].T * grad_scale)[None],
        (home[own : 2 * own] * grad_scale)[None],
        (home[2 * own : 2 * own + 1] + home[2 * own + 1 : 2 * own + 2]) * grad_scale,
    )


def solution(mesh):
    fine = Mesh(mesh.devices.reshape(2, 2, 4, 8, 2), ALL)
    section, fsdp = ("yl", "core"), ("x", "z", "yh")
    in_specs = (
        P(section, fsdp, None),
        P(fsdp, None),
        P(section, None),
        P(section, None, fsdp),
        P(section, fsdp, None),
        P(section, None, fsdp),
        P(section, None, fsdp),
        P(),
        P(),
    )
    out_specs = (
        P(section, fsdp, None),
        P(section, None, fsdp),
        P(section, fsdp, None),
        P(section, None),
    )
    return jax.shard_map(
        on_device, mesh=fine, in_specs=in_specs, out_specs=out_specs, check_vma=False
    )
```

```python
import math

import jax
import jax.numpy as jnp
from jax import lax
from jax.experimental import pallas as pl
from jax.experimental.pallas import tpu as pltpu
from jax.sharding import Mesh, PartitionSpec as P

SAMPLES = 8
COLUMN = ("yl", "core", "z", "yh")
PLANE = ("yl", "core", "x", "yh")
SIDE = 4
ORDER = (2, 1, 3)
PAD = 16
LINES = 8
VMEM_LIMIT = 28 << 20
ALL = ("yl", "core", "x", "z", "yh")


def home_to_work(flip):
    pairs = []
    for i in range(64):
        sec, z2, z10, yh = i >> 4, (i >> 3) & 1, (i >> 1) & 3, i & 1
        pairs.append((i, (z10 << 4) | ((z2 ^ flip) << 3) | (sec << 1) | yh))
    return pairs


def work_to_home(flip):
    return [(j, i) for i, j in home_to_work(flip)]


def next_section():
    return [(z, (z - 1) % 8) for z in range(8)]


def along(stage, shift):
    pairs = []
    for i in range(32):
        yl, core, x, yh = i >> 4, (i >> 3) & 1, (i >> 1) & 3, i & 1
        if (core == 0) == (stage == 1):
            x = (x + shift) % SIDE
        else:
            y = (2 * yh + yl + shift) % SIDE
            yl, yh = y % 2, y // 2
        pairs.append((i, (yl << 4) | (core << 3) | (x << 1) | yh))
    return pairs


def across_cores(value):
    return lax.ppermute(value, "core", [(0, 1), (1, 0)])


def time_features(timestep, freq_width):
    half_width = freq_width // 2
    freq_rates = jnp.exp(
        -math.log(10000.0) * jnp.arange(half_width, dtype=jnp.float32) / half_width
    )
    angles = timestep.astype(jnp.float32)[:, None] * freq_rates[None, :]
    return jnp.concatenate([jnp.cos(angles), jnp.sin(angles)], axis=1).astype(jnp.bfloat16)


def dot_rows(left_side, right_side):
    return lax.dot_general(
        left_side, right_side, (((1,), (1,)), ((), ())), preferred_element_type=jnp.float32
    )


def dot_plain(left_side, right_side):
    return lax.dot_general(
        left_side, right_side, (((1,), (0,)), ((), ())), preferred_element_type=jnp.float32
    )


def dot_first(left_side, right_side):
    return lax.dot_general(
        left_side, right_side, (((0,), (0,)), ((), ())), preferred_element_type=jnp.float32
    )


def two_parts(value):
    high = lax.reduce_precision(value, 8, 7)
    return high.astype(jnp.bfloat16), (value - high).astype(jnp.bfloat16)


def three_parts(value):
    high = lax.reduce_precision(value, 8, 7)
    middle = lax.reduce_precision(value - high, 8, 7)
    return [part.astype(jnp.bfloat16) for part in (high, middle, value - high - middle)]


def row_norm(x_ref):
    inputs = x_ref[...].astype(jnp.float32)
    rscale = lax.rsqrt(jnp.mean(inputs * inputs, axis=1, keepdims=True) + 1e-06)
    return rscale, inputs * rscale


def activation_kernel(
    x_ref, gain_ref, select_ref, b0, b1, w_in_ref, w_out_ref, normed_ref, hidden_ref, slope_ref
):
    rows = (b0.shape[0] // SIDE - LINES) // 2
    for n, block in enumerate((b0, b1)):
        for k in range(SIDE):
            to = pl.ds((n * SIDE + k) * rows, rows)
            w_in_ref[to, :] = block[pl.ds(2 * k * rows, rows), :]
            w_out_ref[to, :] = block[pl.ds((2 * k + 1) * rows, rows), :]
    _, unit = row_norm(x_ref)
    normed = (unit * gain_ref[...]).astype(jnp.bfloat16)
    normed_ref[...] = normed
    tail = pl.ds(2 * SIDE * rows, SIDE * LINES)
    extras = jnp.concatenate([b0[tail, :], b1[tail, :]], axis=0)
    spread = dot_plain(extras, select_ref[...])
    line = lax.broadcasted_iota(jnp.int32, spread.shape, 0)
    shard = lax.broadcasted_iota(jnp.int32, spread.shape, 1) // (rows // 2)
    mine = (line // LINES * 2 + line % LINES == shard) & (line % LINES < 2)
    cond = jnp.sum(jnp.where(mine, spread, 0.0), axis=0, keepdims=True)
    pre = dot_rows(normed, w_in_ref[...]) + cond
    sig = jax.nn.sigmoid(pre)
    hidden_ref[...] = (pre * sig).astype(jnp.bfloat16)
    slope_ref[...] = sig * (1.0 + pre * (1.0 - sig))


def turn_body(g_ref, x_ref, gain_ref, quarters):
    grad = g_ref[...]
    total = None
    pre_grads = []
    for w_in_ref, w_out_ref, slope_ref in quarters:
        pre_grad = dot_rows(grad, w_out_ref[...]) * slope_ref[...]
        pre_grads.append(pre_grad.astype(jnp.bfloat16))
        term = dot_plain(pre_grads[-1], w_in_ref[...])
        total = term if total is None else total + term
    rscale, unit = row_norm(x_ref)
    scaled = total * gain_ref[...]
    inner = jnp.mean(scaled * unit, axis=1, keepdims=True)
    grad_in = grad.astype(jnp.float32) + rscale * (scaled - unit * inner)
    return grad_in.astype(jnp.bfloat16), total * unit, pre_grads


def turn_kernel(g, x, gain, *refs):
    quarters = [refs[i : i + 3] for i in range(0, 12, 3)]
    refs[12][...] = turn_body(g, x, gain, quarters)[0]


def last_turn_kernel(g, x, gain, *refs):
    quarters = [refs[i : i + 3] for i in range(0, 12, 3)]
    out, gain_out = refs[12:14]
    grad_in, terms, pre_grads = turn_body(g, x, gain, quarters)
    out[...] = grad_in
    gain_out[...] = jnp.sum(terms, axis=0, keepdims=True)
    for ref, pre_grad in zip(refs[14:], pre_grads):
        ref[...] = pre_grad


def outer_kernel(left_0, left_1, right, out):
    for n, left in enumerate((left_0, left_1)):
        rows = pl.ds(n * left.shape[1], left.shape[1])
        out[rows, :] = dot_first(left[...], right[...]).astype(jnp.bfloat16)


def copy_kernel(value, out):
    out[...] = value[...]


def high_low_rows(value):
    line = lax.broadcasted_iota(jnp.int32, (PAD, value.shape[1]), 0)
    high = value.astype(jnp.bfloat16).astype(jnp.float32)
    rows = jnp.where(line == 0, high, jnp.where(line == 1, value - high, 0.0))
    return rows.astype(jnp.bfloat16)


def near_kernel(
    pg_0, pg_1, normed, in_far, hidden_0, hidden_1, grad, out_far, gain_here, gain_there, *sums
):
    rows = (sums[0].shape[0] - PAD) // SIDE // 2
    products = (((pg_0, pg_1), normed, in_far), ((hidden_0, hidden_1), grad, out_far))
    for first, (lefts, right, far) in enumerate(products):
        for n, left in enumerate(lefts):
            width = left.shape[1]
            total = dot_first(left[...], right[...])
            total = total + far[pl.ds(n * width, width), :].astype(jnp.float32)
            total = total.astype(jnp.bfloat16)
            for k in range(width // rows):
                peer = n * width // rows + k
                to = pl.ds((peer % SIDE * 2 + first) * rows, rows)
                sums[peer // SIDE][to, :] = total[k * rows : (k + 1) * rows, :]
    gain = high_low_rows(gain_here[...] + gain_there[...])
    for out in sums:
        out[pl.ds(out.shape[0] - PAD, PAD), :] = gain


def stage_sum_kernel(s0, s1, s2, s3, *outs):
    rows = outs[0].shape[0] - PAD
    for k, out in enumerate(outs):
        cut = pl.ds(k * rows, rows)
        total = sum(s[cut, :].astype(jnp.float32) for s in (s0, s1, s2, s3))
        out[pl.ds(0, rows), :] = total.astype(jnp.bfloat16)
    tail = pl.ds(s0.shape[0] - PAD, PAD)
    total = sum(s[tail, :].astype(jnp.float32) for s in (s0, s1, s2, s3))
    gain = high_low_rows(jnp.sum(total, axis=0, keepdims=True))
    for out in outs:
        out[pl.ds(rows, PAD), :] = gain


def kernel(body, outs, flops=0):
    whole = pl.BlockSpec(memory_space=pltpu.VMEM)
    shapes = [jax.ShapeDtypeStruct(*out) for out in outs]

    def call(*operands):
        result = pl.pallas_call(
            body,
            out_shape=shapes,
            in_specs=[whole] * len(operands),
            out_specs=[whole] * len(shapes),
            compiler_params=pltpu.CompilerParams(vmem_limit_bytes=VMEM_LIMIT),
            cost_estimate=pl.CostEstimate(flops=flops, bytes_accessed=4 << 20, transcendentals=0),
        )(*operands)
        return result if len(shapes) > 1 else result[0]

    return call


def on_device(checkpoints, cotangent, gains, w_in, w_out, time_proj, class_table, timestep, label):
    rows, chan = checkpoints.shape[1:]
    own = w_in.shape[2]
    half = SIDE * SIDE * 2 * own
    grad_scale = float(rows * 64) ** (-0.5)
    sample = 2 * lax.axis_index("x") + lax.axis_index("z") // 4
    bf16, f32 = jnp.bfloat16, jnp.float32

    time_feats = time_features(timestep, time_proj.shape[1])
    picks = (
        label[:, None] == jnp.arange(class_table.shape[1], dtype=jnp.int32)[None, :]
    ).astype(bf16)
    cond = dot_plain(time_feats, time_proj[0]) + dot_plain(picks, class_table[0])
    cond_row = jnp.concatenate([part.reshape(1, -1) for part in two_parts(cond)], axis=1)
    line = jnp.arange(8, dtype=jnp.int32)[:, None]
    spare = jnp.zeros((8, chan), bf16)
    for n, row in enumerate((cond_row, *three_parts(gains))):
        spare = jnp.where(line == n, row, spare)
    shard = jnp.concatenate([w_in[0].T, w_out[0], spare], axis=0)

    one, two = (lax.ppermute(shard, COLUMN, home_to_work(flip)) for flip in (0, 1))
    chunk = jnp.concatenate(
        [
            one[:own],
            two[:own],
            one[own : 2 * own],
            two[own : 2 * own],
            one[2 * own : 2 * own + 1],
            two[2 * own : 2 * own + 1],
            jnp.zeros((LINES - 2, chan), bf16),
        ],
        axis=0,
    )
    chunk, x_rows = lax.optimization_barrier((chunk, checkpoints[0]))
    x_rows = lax.ppermute(x_rows, COLUMN, home_to_work(0))
    chunks = [chunk] + [lax.ppermute(chunk, PLANE, along(1, k)) for k in range(1, SIDE)]
    quarter = jnp.concatenate(
        [part[: 4 * own] for part in chunks] + [part[4 * own :] for part in chunks], axis=0
    )
    quarter, x_rows = lax.optimization_barrier((quarter, x_rows))
    gain_row = one[2 * own + 1 : 2 * own + 4].astype(f32)
    gain_row = gain_row[0:1] + gain_row[1:2] + gain_row[2:3]
    near = [quarter] + [lax.ppermute(quarter, PLANE, along(2, k)) for k in ORDER]
    cotangent, near[1] = lax.optimization_barrier((cotangent, near[1]))
    cot_rows = lax.ppermute(
        cotangent, COLUMN, [pair for pair in home_to_work(0) if pair[0] >> 4 == 3]
    )

    width = half // 2
    entry = jnp.arange(chan, dtype=jnp.int32)[:, None]
    hidden_col = jnp.arange(width, dtype=jnp.int32)[None, :]
    select = (
        (entry % own == hidden_col % own) & (entry // own % SAMPLES == sample)
    ).astype(bf16)

    flops = 2 * rows * half * chan
    activate = kernel(
        activation_kernel,
        [
            ((width, chan), bf16),
            ((width, chan), bf16),
            ((rows, chan), bf16),
            ((rows, width), bf16),
            ((rows, width), f32),
        ],
        flops,
    )
    first_far = [across_cores(block) for block in near[:2]]
    first = [activate(x_rows, gain_row, select, *blocks) for blocks in (near[:2], first_far)]
    last_near, cot_rows, *first = lax.optimization_barrier((near[3], cot_rows, *first))
    near, last_far = [near[2], last_near], [across_cores(near[2]), across_cores(last_near)]
    second = [activate(x_rows, gain_row, select, *blocks) for blocks in (near, last_far)]
    quarters = [first[0], second[0], first[1], second[1]]
    normed = quarters[0][2]
    hiddens = [quarter[3] for quarter in quarters]
    held = [x_rows, gain_row]
    for w_in_rows, w_out_rows, _, _, slope in quarters:
        held += [w_in_rows, w_out_rows, slope]

    turn = kernel(turn_kernel, [((rows, chan), bf16)], 4 * flops)
    kept = grad = cot_rows
    for _ in range(3):
        grad = lax.ppermute(turn(grad, *held), "z", next_section())
        kept = kept + grad

    outer = kernel(outer_kernel, [((half, chan), bf16)], flops)
    far_out = outer(*hiddens[2:], kept)
    kept, far_out = lax.optimization_barrier((kept, far_out))
    recv_out = across_cores(far_out)
    last_turn = kernel(
        last_turn_kernel,
        [((rows, chan), bf16), ((1, chan), f32)] + [((rows, width), bf16)] * 4,
        4 * flops,
    )
    grad_in, gain_part, pg_0, pg_1, *pg_far = last_turn(kept, *held)
    *pg_far, recv_out = lax.optimization_barrier((*pg_far, recv_out))
    recv_in = across_cores(outer(*pg_far, normed))
    gain_there = across_cores(gain_part)
    sums = kernel(near_kernel, [((SIDE * 4 * own + PAD, chan), bf16)] * SIDE, 2 * flops)(
        pg_0, pg_1, normed, recv_in, *hiddens[:2], kept, recv_out, gain_part, gain_there
    )
    grad_home = lax.ppermute(grad_in, COLUMN, work_to_home(0))
    grad_home = kernel(copy_kernel, [((rows, chan), bf16)])(grad_home)

    parts = [sums[0]] + [
        lax.ppermute(part, PLANE, along(2, SIDE - k)) for k, part in zip(ORDER, sums[1:])
    ]
    *parts, grad_home = lax.optimization_barrier((*parts, grad_home))
    sums = kernel(stage_sum_kernel, [((4 * own + PAD, chan), bf16)] * SIDE)(*parts)
    parts = [sums[0]] + [
        lax.ppermute(part, PLANE, along(1, SIDE - k)) for k, part in enumerate(sums[1:], 1)
    ]
    total = sum(part.astype(f32) for part in parts)
    gain_lines = list(two_parts(total[4 * own : 4 * own + 1] + total[4 * own + 1 : 4 * own + 2]))
    gain_lines.append(jnp.zeros((6, chan), bf16))
    total = total.astype(bf16)
    home = sum(
        lax.ppermute(
            jnp.concatenate(
                [
                    total[flip * own : (flip + 1) * own],
                    total[(2 + flip) * own : (3 + flip) * own],
                    *gain_lines,
                ],
                axis=0,
            ),
            COLUMN,
            work_to_home(flip),
        ).astype(f32)
        for flip in (0, 1)
    )
    return (
        grad_home[None],
        (home[:own].T * grad_scale)[None],
        (home[own : 2 * own] * grad_scale)[None],
        (home[2 * own : 2 * own + 1] + home[2 * own + 1 : 2 * own + 2]) * grad_scale,
    )


def solution(mesh):
    fine = Mesh(mesh.devices.reshape(2, 2, 4, 8, 2), ALL)
    section, fsdp = ("yl", "core"), ("x", "z", "yh")
    in_specs = (
        P(section, fsdp, None),
        P(fsdp, None),
        P(section, None),
        P(section, None, fsdp),
        P(section, fsdp, None),
        P(section, None, fsdp),
        P(section, None, fsdp),
        P(),
        P(),
    )
    out_specs = (
        P(section, fsdp, None),
        P(section, None, fsdp),
        P(section, fsdp, None),
        P(section, None),
    )
    return jax.shard_map(
        on_device, mesh=fine, in_specs=in_specs, out_specs=out_specs, check_vma=False
    )
```

```python
import math

import jax
import jax.numpy as jnp
from jax import lax
from jax.experimental import pallas as pl
from jax.experimental.pallas import tpu as pltpu
from jax.sharding import Mesh, PartitionSpec as P

SAMPLES = 8
COLUMN = ("yl", "core", "z", "yh")
PLANE = ("yl", "core", "x", "yh")
SIDE = 4
ORDER = (2, 1, 3)
GRAD_SCALE = 8192.0 ** (-0.5)
PAD = 16
LINES = 8
VMEM_LIMIT = 28 << 20
ALL = ("yl", "core", "x", "z", "yh")


def home_to_work(flip):
    pairs = []
    for i in range(64):
        sec, z2, z10, yh = i >> 4, (i >> 3) & 1, (i >> 1) & 3, i & 1
        pairs.append((i, (z10 << 4) | ((z2 ^ flip) << 3) | (sec << 1) | yh))
    return pairs


def work_to_home(flip):
    return [(j, i) for i, j in home_to_work(flip)]


def next_section():
    return [(z, (z - 1) % 8) for z in range(8)]


def along(stage, shift):
    pairs = []
    for i in range(32):
        yl, core, x, yh = i >> 4, (i >> 3) & 1, (i >> 1) & 3, i & 1
        if (core == 0) == (stage == 1):
            x = (x + shift) % SIDE
        else:
            y = (2 * yh + yl + shift) % SIDE
            yl, yh = y % 2, y // 2
        pairs.append((i, (yl << 4) | (core << 3) | (x << 1) | yh))
    return pairs


def across_cores(value):
    return lax.ppermute(value, "core", [(0, 1), (1, 0)])


def time_features(timestep, freq_width):
    half_width = freq_width // 2
    freq_rates = jnp.exp(
        -math.log(10000.0) * jnp.arange(half_width, dtype=jnp.float32) / half_width
    )
    angles = timestep.astype(jnp.float32)[:, None] * freq_rates[None, :]
    return jnp.concatenate([jnp.cos(angles), jnp.sin(angles)], axis=1).astype(jnp.bfloat16)


def dot_rows(left_side, right_side):
    return lax.dot_general(
        left_side, right_side, (((1,), (1,)), ((), ())), preferred_element_type=jnp.float32
    )


def dot_plain(left_side, right_side):
    return lax.dot_general(
        left_side, right_side, (((1,), (0,)), ((), ())), preferred_element_type=jnp.float32
    )


def dot_first(left_side, right_side):
    return lax.dot_general(
        left_side, right_side, (((0,), (0,)), ((), ())), preferred_element_type=jnp.float32
    )


def two_parts(value):
    high = lax.reduce_precision(value, 8, 7)
    return high.astype(jnp.bfloat16), (value - high).astype(jnp.bfloat16)


def three_parts(value):
    high = lax.reduce_precision(value, 8, 7)
    middle = lax.reduce_precision(value - high, 8, 7)
    return [part.astype(jnp.bfloat16) for part in (high, middle, value - high - middle)]


def row_norm(x_ref):
    inputs = x_ref[...].astype(jnp.float32)
    rscale = lax.rsqrt(jnp.mean(inputs * inputs, axis=1, keepdims=True) + 1e-06)
    return rscale, inputs * rscale


def activation_kernel(
    x_ref, gain_ref, select_ref, b0, b1, w_in_ref, w_out_ref, normed_ref, hidden_ref, slope_ref
):
    rows = (b0.shape[0] // SIDE - LINES) // 2
    for n, block in enumerate((b0, b1)):
        for k in range(SIDE):
            to = pl.ds((n * SIDE + k) * rows, rows)
            w_in_ref[to, :] = block[pl.ds(2 * k * rows, rows), :]
            w_out_ref[to, :] = block[pl.ds((2 * k + 1) * rows, rows), :]
    _, unit = row_norm(x_ref)
    normed = (unit * gain_ref[...]).astype(jnp.bfloat16)
    normed_ref[...] = normed
    tail = pl.ds(2 * SIDE * rows, SIDE * LINES)
    extras = jnp.concatenate([b0[tail, :], b1[tail, :]], axis=0)
    spread = dot_plain(extras, select_ref[...])
    line = lax.broadcasted_iota(jnp.int32, spread.shape, 0)
    shard = lax.broadcasted_iota(jnp.int32, spread.shape, 1) // (rows // 2)
    mine = (line // LINES * 2 + line % LINES == shard) & (line % LINES < 2)
    cond = jnp.sum(jnp.where(mine, spread, 0.0), axis=0, keepdims=True)
    pre = dot_rows(normed, w_in_ref[...]) + cond
    sig = jax.nn.sigmoid(pre)
    hidden_ref[...] = (pre * sig).astype(jnp.bfloat16)
    slope_ref[...] = sig * (1.0 + pre * (1.0 - sig))


def turn_body(g_ref, x_ref, gain_ref, quarters):
    grad = g_ref[...]
    total = None
    pre_grads = []
    for w_in_ref, w_out_ref, slope_ref in quarters:
        pre_grad = dot_rows(grad, w_out_ref[...]) * slope_ref[...]
        pre_grads.append(pre_grad.astype(jnp.bfloat16))
        term = dot_plain(pre_grads[-1], w_in_ref[...])
        total = term if total is None else total + term
    rscale, unit = row_norm(x_ref)
    scaled = total * gain_ref[...]
    inner = jnp.mean(scaled * unit, axis=1, keepdims=True)
    grad_in = grad.astype(jnp.float32) + rscale * (scaled - unit * inner)
    return grad_in.astype(jnp.bfloat16), total * unit, pre_grads


def turn_kernel(g, x, gain, *refs):
    quarters = [refs[i : i + 3] for i in range(0, 12, 3)]
    refs[12][...] = turn_body(g, x, gain, quarters)[0]


def last_turn_kernel(g, x, gain, *refs):
    quarters = [refs[i : i + 3] for i in range(0, 12, 3)]
    out, gain_out = refs[12:14]
    grad_in, terms, pre_grads = turn_body(g, x, gain, quarters)
    out[...] = grad_in
    gain_out[...] = jnp.sum(terms, axis=0, keepdims=True)
    for ref, pre_grad in zip(refs[14:], pre_grads):
        ref[...] = pre_grad


def outer_kernel(left_0, left_1, right, out):
    for n, left in enumerate((left_0, left_1)):
        rows = pl.ds(n * left.shape[1], left.shape[1])
        out[rows, :] = dot_first(left[...], right[...]).astype(jnp.bfloat16)


def first_outer_kernel(left_0, left_1, earlier, last, out, kept):
    kept[...] = earlier[...] + last[...]
    outer_kernel(left_0, left_1, kept, out)


def home_kernel(part_0, part_1, w_in_out, w_out_out, gain_out):
    own = w_in_out.shape[0]
    total = (part_0[...].astype(jnp.float32) + part_1[...].astype(jnp.float32)) * GRAD_SCALE
    w_in_out[...] = total[:own, :]
    w_out_out[...] = total[own : 2 * own, :]
    gain_out[...] = total[2 * own : 2 * own + 1, :] + total[2 * own + 1 : 2 * own + 2, :]


def copy_kernel(value, out):
    out[...] = value[...]


def high_low_rows(value):
    line = lax.broadcasted_iota(jnp.int32, (PAD, value.shape[1]), 0)
    high = value.astype(jnp.bfloat16).astype(jnp.float32)
    rows = jnp.where(line == 0, high, jnp.where(line == 1, value - high, 0.0))
    return rows.astype(jnp.bfloat16)


def near_kernel(
    pg_0, pg_1, normed, in_far, hidden_0, hidden_1, grad, out_far, gain_here, gain_there, *sums
):
    rows = (sums[0].shape[0] - PAD) // SIDE // 2
    products = (((pg_0, pg_1), normed, in_far), ((hidden_0, hidden_1), grad, out_far))
    for first, (lefts, right, far) in enumerate(products):
        for n, left in enumerate(lefts):
            width = left.shape[1]
            total = dot_first(left[...], right[...])
            total = total + far[pl.ds(n * width, width), :].astype(jnp.float32)
            total = total.astype(jnp.bfloat16)
            for k in range(width // rows):
                peer = n * width // rows + k
                to = pl.ds((peer % SIDE * 2 + first) * rows, rows)
                sums[peer // SIDE][to, :] = total[k * rows : (k + 1) * rows, :]
    gain = high_low_rows(gain_here[...] + gain_there[...])
    for out in sums:
        out[pl.ds(out.shape[0] - PAD, PAD), :] = gain


def stage_sum_kernel(s0, s1, s2, s3, *outs):
    rows = outs[0].shape[0] - PAD
    for k, out in enumerate(outs):
        cut = pl.ds(k * rows, rows)
        total = sum(s[cut, :].astype(jnp.float32) for s in (s0, s1, s2, s3))
        out[pl.ds(0, rows), :] = total.astype(jnp.bfloat16)
    tail = pl.ds(s0.shape[0] - PAD, PAD)
    total = sum(s[tail, :].astype(jnp.float32) for s in (s0, s1, s2, s3))
    gain = high_low_rows(jnp.sum(total, axis=0, keepdims=True))
    for out in outs:
        out[pl.ds(rows, PAD), :] = gain


def kernel(body, outs, flops=0):
    whole = pl.BlockSpec(memory_space=pltpu.VMEM)
    shapes = [jax.ShapeDtypeStruct(*out) for out in outs]

    def call(*operands):
        result = pl.pallas_call(
            body,
            out_shape=shapes,
            in_specs=[whole] * len(operands),
            out_specs=[whole] * len(shapes),
            compiler_params=pltpu.CompilerParams(vmem_limit_bytes=VMEM_LIMIT),
            cost_estimate=pl.CostEstimate(flops=flops, bytes_accessed=4 << 20, transcendentals=0),
        )(*operands)
        return result if len(shapes) > 1 else result[0]

    return call


def on_device(checkpoints, cotangent, gains, w_in, w_out, time_proj, class_table, timestep, label):
    rows, chan = checkpoints.shape[1:]
    own = w_in.shape[2]
    half = SIDE * SIDE * 2 * own
    sample = 2 * lax.axis_index("x") + lax.axis_index("z") // 4
    bf16, f32 = jnp.bfloat16, jnp.float32

    time_feats = time_features(timestep, time_proj.shape[1])
    picks = (
        label[:, None] == jnp.arange(class_table.shape[1], dtype=jnp.int32)[None, :]
    ).astype(bf16)
    cond = dot_plain(time_feats, time_proj[0]) + dot_plain(picks, class_table[0])
    cond_row = jnp.concatenate([part.reshape(1, -1) for part in two_parts(cond)], axis=1)
    line = jnp.arange(8, dtype=jnp.int32)[:, None]
    spare = jnp.zeros((8, chan), bf16)
    for n, row in enumerate((cond_row, *three_parts(gains))):
        spare = jnp.where(line == n, row, spare)
    shard = jnp.concatenate([w_in[0].T, w_out[0], spare], axis=0)

    one, two = (lax.ppermute(shard, COLUMN, home_to_work(flip)) for flip in (0, 1))
    chunk = jnp.concatenate(
        [
            one[:own],
            two[:own],
            one[own : 2 * own],
            two[own : 2 * own],
            one[2 * own : 2 * own + 1],
            two[2 * own : 2 * own + 1],
            jnp.zeros((LINES - 2, chan), bf16),
        ],
        axis=0,
    )
    chunk, x_rows = lax.optimization_barrier((chunk, checkpoints[0]))
    x_rows = lax.ppermute(x_rows, COLUMN, home_to_work(0))
    chunks = [chunk] + [lax.ppermute(chunk, PLANE, along(1, k)) for k in range(1, SIDE)]
    quarter = jnp.concatenate(
        [part[: 4 * own] for part in chunks] + [part[4 * own :] for part in chunks], axis=0
    )
    quarter, x_rows = lax.optimization_barrier((quarter, x_rows))
    gain_row = one[2 * own + 1 : 2 * own + 4].astype(f32)
    gain_row = gain_row[0:1] + gain_row[1:2] + gain_row[2:3]
    near = [quarter] + [lax.ppermute(quarter, PLANE, along(2, k)) for k in ORDER]
    cotangent, near[1] = lax.optimization_barrier((cotangent, near[1]))
    cot_rows = lax.ppermute(
        cotangent, COLUMN, [pair for pair in home_to_work(0) if pair[0] >> 4 == 3]
    )

    width = half // 2
    entry = jnp.arange(chan, dtype=jnp.int32)[:, None]
    hidden_col = jnp.arange(width, dtype=jnp.int32)[None, :]
    select = (
        (entry % own == hidden_col % own) & (entry // own % SAMPLES == sample)
    ).astype(bf16)

    flops = 2 * rows * half * chan
    activate = kernel(
        activation_kernel,
        [
            ((width, chan), bf16),
            ((width, chan), bf16),
            ((rows, chan), bf16),
            ((rows, width), bf16),
            ((rows, width), f32),
        ],
        flops,
    )
    first_far = [across_cores(block) for block in near[:2]]
    first = [activate(x_rows, gain_row, select, *blocks) for blocks in (near[:2], first_far)]
    last_near, cot_rows, *first = lax.optimization_barrier((near[3], cot_rows, *first))
    near, last_far = [near[2], last_near], [across_cores(near[2]), across_cores(last_near)]
    second = [activate(x_rows, gain_row, select, *blocks) for blocks in (near, last_far)]
    quarters = [first[0], second[0], first[1], second[1]]
    normed = quarters[0][2]
    hiddens = [quarter[3] for quarter in quarters]
    held = [x_rows, gain_row]
    for w_in_rows, w_out_rows, _, _, slope in quarters:
        held += [w_in_rows, w_out_rows, slope]

    turn = kernel(turn_kernel, [((rows, chan), bf16)], 4 * flops)
    grad, earlier = cot_rows, jnp.zeros_like(cot_rows)
    for _ in range(3):
        earlier = earlier + grad
        grad = lax.ppermute(turn(grad, *held), "z", next_section())

    far_out, kept = kernel(
        first_outer_kernel, [((half, chan), bf16), ((rows, chan), bf16)], flops
    )(*hiddens[2:], earlier, grad)
    kept, far_out = lax.optimization_barrier((kept, far_out))
    recv_out = across_cores(far_out)
    last_turn = kernel(
        last_turn_kernel,
        [((rows, chan), bf16), ((1, chan), f32)] + [((rows, width), bf16)] * 4,
        4 * flops,
    )
    grad_in, gain_part, pg_0, pg_1, *pg_far = last_turn(kept, *held)
    far_in = kernel(outer_kernel, [((half, chan), bf16)], flops)(*pg_far, normed)
    far_in, recv_out = lax.optimization_barrier((far_in, recv_out))
    recv_in = across_cores(far_in)
    gain_there = across_cores(gain_part)
    sums = kernel(near_kernel, [((SIDE * 4 * own + PAD, chan), bf16)] * SIDE, 2 * flops)(
        pg_0, pg_1, normed, recv_in, *hiddens[:2], kept, recv_out, gain_part, gain_there
    )
    grad_home = lax.ppermute(grad_in, COLUMN, work_to_home(0))
    grad_home = kernel(copy_kernel, [((rows, chan), bf16)])(grad_home)

    parts = [sums[0]] + [
        lax.ppermute(part, PLANE, along(2, SIDE - k)) for k, part in zip(ORDER, sums[1:])
    ]
    *parts, grad_home = lax.optimization_barrier((*parts, grad_home))
    sums = kernel(stage_sum_kernel, [((4 * own + PAD, chan), bf16)] * SIDE)(*parts)
    parts = [sums[0]] + [
        lax.ppermute(part, PLANE, along(1, SIDE - k)) for k, part in enumerate(sums[1:], 1)
    ]
    total = sum(part.astype(f32) for part in parts)
    gain_lines = list(two_parts(total[4 * own : 4 * own + 1] + total[4 * own + 1 : 4 * own + 2]))
    gain_lines.append(jnp.zeros((6, chan), bf16))
    total = total.astype(bf16)
    parts = [
        lax.ppermute(
            jnp.concatenate(
                [
                    total[flip * own : (flip + 1) * own],
                    total[(2 + flip) * own : (3 + flip) * own],
                    *gain_lines,
                ],
                axis=0,
            ),
            COLUMN,
            work_to_home(flip),
        )
        for flip in (0, 1)
    ]
    w_in_home, w_out_home, gain_home = kernel(
        home_kernel, [((own, chan), f32), ((own, chan), f32), ((1, chan), f32)]
    )(*parts)
    return grad_home[None], w_in_home.T[None], w_out_home[None], gain_home


def solution(mesh):
    fine = Mesh(mesh.devices.reshape(2, 2, 4, 8, 2), ALL)
    section, fsdp = ("yl", "core"), ("x", "z", "yh")
    in_specs = (
        P(section, fsdp, None),
        P(fsdp, None),
        P(section, None),
        P(section, None, fsdp),
        P(section, fsdp, None),
        P(section, None, fsdp),
        P(section, None, fsdp),
        P(),
        P(),
    )
    out_specs = (
        P(section, fsdp, None),
        P(section, None, fsdp),
        P(section, fsdp, None),
        P(section, None),
    )
    return jax.shard_map(
        on_device, mesh=fine, in_specs=in_specs, out_specs=out_specs, check_vma=False
    )
```

```python
import math

import jax
import jax.numpy as jnp
from jax import lax
from jax.experimental import pallas as pl
from jax.experimental.pallas import tpu as pltpu
from jax.sharding import Mesh, PartitionSpec as P

SAMPLES = 8
COLUMN = ("yl", "core", "z", "yh")
PLANE = ("yl", "core", "x", "yh")
SIDE = 4
ORDER = (2, 1, 3)
GRAD_SCALE = 8192.0 ** (-0.5)
PAD = 16
LINES = 8
VMEM_LIMIT = 28 << 20
ALL = ("yl", "core", "x", "z", "yh")


def home_to_work(flip):
    pairs = []
    for i in range(64):
        sec, z2, z10, yh = i >> 4, (i >> 3) & 1, (i >> 1) & 3, i & 1
        pairs.append((i, (z10 << 4) | ((z2 ^ flip) << 3) | (sec << 1) | yh))
    return pairs


def work_to_home(flip):
    return [(j, i) for i, j in home_to_work(flip)]


def next_section():
    return [(z, (z - 1) % 8) for z in range(8)]


def along(stage, shift):
    pairs = []
    for i in range(32):
        yl, core, x, yh = i >> 4, (i >> 3) & 1, (i >> 1) & 3, i & 1
        if (core == 0) == (stage == 1):
            x = (x + shift) % SIDE
        else:
            y = (2 * yh + yl + shift) % SIDE
            yl, yh = y % 2, y // 2
        pairs.append((i, (yl << 4) | (core << 3) | (x << 1) | yh))
    return pairs


def across_cores(value):
    return lax.ppermute(value, "core", [(0, 1), (1, 0)])


def time_features(timestep, freq_width):
    half_width = freq_width // 2
    freq_rates = jnp.exp(
        -math.log(10000.0) * jnp.arange(half_width, dtype=jnp.float32) / half_width
    )
    angles = timestep.astype(jnp.float32)[:, None] * freq_rates[None, :]
    return jnp.concatenate([jnp.cos(angles), jnp.sin(angles)], axis=1).astype(jnp.bfloat16)


def dot_rows(left_side, right_side):
    return lax.dot_general(
        left_side, right_side, (((1,), (1,)), ((), ())), preferred_element_type=jnp.float32
    )


def dot_plain(left_side, right_side):
    return lax.dot_general(
        left_side, right_side, (((1,), (0,)), ((), ())), preferred_element_type=jnp.float32
    )


def dot_first(left_side, right_side):
    return lax.dot_general(
        left_side, right_side, (((0,), (0,)), ((), ())), preferred_element_type=jnp.float32
    )


def two_parts(value):
    high = lax.reduce_precision(value, 8, 7)
    return high.astype(jnp.bfloat16), (value - high).astype(jnp.bfloat16)


def three_parts(value):
    high = lax.reduce_precision(value, 8, 7)
    middle = lax.reduce_precision(value - high, 8, 7)
    return [part.astype(jnp.bfloat16) for part in (high, middle, value - high - middle)]


def row_norm(x_ref):
    inputs = x_ref[...].astype(jnp.float32)
    rscale = lax.rsqrt(jnp.mean(inputs * inputs, axis=1, keepdims=True) + 1e-06)
    return rscale, inputs * rscale


def activation_kernel(
    x_ref, gain_ref, select_ref, b0, b1, w_in_ref, w_out_ref, normed_ref, hidden_ref, slope_ref
):
    rows = (b0.shape[0] // SIDE - LINES) // 2
    for n, block in enumerate((b0, b1)):
        for k in range(SIDE):
            to = pl.ds((n * SIDE + k) * rows, rows)
            w_in_ref[to, :] = block[pl.ds(2 * k * rows, rows), :]
            w_out_ref[to, :] = block[pl.ds((2 * k + 1) * rows, rows), :]
    _, unit = row_norm(x_ref)
    normed = (unit * gain_ref[...]).astype(jnp.bfloat16)
    normed_ref[...] = normed
    tail = pl.ds(2 * SIDE * rows, SIDE * LINES)
    extras = jnp.concatenate([b0[tail, :], b1[tail, :]], axis=0)
    spread = dot_plain(extras, select_ref[...])
    line = lax.broadcasted_iota(jnp.int32, spread.shape, 0)
    shard = lax.broadcasted_iota(jnp.int32, spread.shape, 1) // (rows // 2)
    mine = (line // LINES * 2 + line % LINES == shard) & (line % LINES < 2)
    cond = jnp.sum(jnp.where(mine, spread, 0.0), axis=0, keepdims=True)
    pre = dot_rows(normed, w_in_ref[...]) + cond
    sig = jax.nn.sigmoid(pre)
    hidden_ref[...] = (pre * sig).astype(jnp.bfloat16)
    slope_ref[...] = sig * (1.0 + pre * (1.0 - sig))


def turn_body(g_ref, x_ref, gain_ref, quarters):
    grad = g_ref[...]
    total = None
    pre_grads = []
    for w_in_ref, w_out_ref, slope_ref in quarters:
        pre_grad = dot_rows(grad, w_out_ref[...]) * slope_ref[...]
        pre_grads.append(pre_grad.astype(jnp.bfloat16))
        term = dot_plain(pre_grads[-1], w_in_ref[...])
        total = term if total is None else total + term
    rscale, unit = row_norm(x_ref)
    scaled = total * gain_ref[...]
    inner = jnp.mean(scaled * unit, axis=1, keepdims=True)
    grad_in = grad.astype(jnp.float32) + rscale * (scaled - unit * inner)
    return grad_in.astype(jnp.bfloat16), total * unit, pre_grads


def turn_kernel(g, x, gain, *refs):
    quarters = [refs[i : i + 3] for i in range(0, 12, 3)]
    refs[12][...] = turn_body(g, x, gain, quarters)[0]


def last_turn_kernel(g, x, gain, *refs):
    quarters = [refs[i : i + 3] for i in range(0, 12, 3)]
    out, gain_out = refs[12:14]
    grad_in, terms, pre_grads = turn_body(g, x, gain, quarters)
    out[...] = grad_in
    gain_out[...] = jnp.sum(terms, axis=0, keepdims=True)
    for ref, pre_grad in zip(refs[14:], pre_grads):
        ref[...] = pre_grad


def outer_kernel(left_0, left_1, right, out):
    for n, left in enumerate((left_0, left_1)):
        rows = pl.ds(n * left.shape[1], left.shape[1])
        out[rows, :] = dot_first(left[...], right[...]).astype(jnp.bfloat16)


def first_outer_kernel(left_0, left_1, earlier, last, out, kept):
    kept[...] = earlier[...] + last[...]
    outer_kernel(left_0, left_1, kept, out)


def home_kernel(part_0, part_1, w_in_out, w_out_out, gain_out):
    own = w_in_out.shape[0]
    total = (part_0[...].astype(jnp.float32) + part_1[...].astype(jnp.float32)) * GRAD_SCALE
    w_in_out[...] = total[:own, :]
    w_out_out[...] = total[own : 2 * own, :]
    gain_out[...] = total[2 * own : 2 * own + 1, :] + total[2 * own + 1 : 2 * own + 2, :]


def copy_kernel(value, out):
    out[...] = value[...]


def high_low_rows(value):
    line = lax.broadcasted_iota(jnp.int32, (PAD, value.shape[1]), 0)
    high = value.astype(jnp.bfloat16).astype(jnp.float32)
    rows = jnp.where(line == 0, high, jnp.where(line == 1, value - high, 0.0))
    return rows.astype(jnp.bfloat16)


def near_kernel(
    pg_0, pg_1, normed, in_far, hidden_0, hidden_1, grad, out_far, gain_here, gain_there, *sums
):
    rows = (sums[0].shape[0] - PAD) // SIDE // 2
    products = (((pg_0, pg_1), normed, in_far), ((hidden_0, hidden_1), grad, out_far))
    for first, (lefts, right, far) in enumerate(products):
        for n, left in enumerate(lefts):
            width = left.shape[1]
            total = dot_first(left[...], right[...])
            total = total + far[pl.ds(n * width, width), :].astype(jnp.float32)
            total = total.astype(jnp.bfloat16)
            for k in range(width // rows):
                peer = n * width // rows + k
                to = pl.ds((peer % SIDE * 2 + first) * rows, rows)
                sums[peer // SIDE][to, :] = total[k * rows : (k + 1) * rows, :]
    gain = high_low_rows(gain_here[...] + gain_there[...])
    for out in sums:
        out[pl.ds(out.shape[0] - PAD, PAD), :] = gain


def stage_sum_kernel(s0, s1, s2, s3, *outs):
    rows = outs[0].shape[0] - PAD
    for k, out in enumerate(outs):
        cut = pl.ds(k * rows, rows)
        total = sum(s[cut, :].astype(jnp.float32) for s in (s0, s1, s2, s3))
        out[pl.ds(0, rows), :] = total.astype(jnp.bfloat16)
    tail = pl.ds(s0.shape[0] - PAD, PAD)
    total = sum(s[tail, :].astype(jnp.float32) for s in (s0, s1, s2, s3))
    gain = high_low_rows(jnp.sum(total, axis=0, keepdims=True))
    for out in outs:
        out[pl.ds(rows, PAD), :] = gain


def kernel(body, outs, flops=0):
    whole = pl.BlockSpec(memory_space=pltpu.VMEM)
    shapes = [jax.ShapeDtypeStruct(*out) for out in outs]

    def call(*operands):
        result = pl.pallas_call(
            body,
            out_shape=shapes,
            in_specs=[whole] * len(operands),
            out_specs=[whole] * len(shapes),
            compiler_params=pltpu.CompilerParams(vmem_limit_bytes=VMEM_LIMIT),
            cost_estimate=pl.CostEstimate(flops=flops, bytes_accessed=4 << 20, transcendentals=0),
        )(*operands)
        return result if len(shapes) > 1 else result[0]

    return call


def on_device(checkpoints, cotangent, gains, w_in, w_out, time_proj, class_table, timestep, label):
    rows, chan = checkpoints.shape[1:]
    own = w_in.shape[2]
    half = SIDE * SIDE * 2 * own
    sample = 2 * lax.axis_index("x") + lax.axis_index("z") // 4
    bf16, f32 = jnp.bfloat16, jnp.float32

    time_feats = time_features(timestep, time_proj.shape[1])
    picks = (
        label[:, None] == jnp.arange(class_table.shape[1], dtype=jnp.int32)[None, :]
    ).astype(bf16)
    cond = dot_plain(time_feats, time_proj[0]) + dot_plain(picks, class_table[0])
    cond_row = jnp.concatenate([part.reshape(1, -1) for part in two_parts(cond)], axis=1)
    line = jnp.arange(8, dtype=jnp.int32)[:, None]
    spare = jnp.zeros((8, chan), bf16)
    for n, row in enumerate((cond_row, *three_parts(gains))):
        spare = jnp.where(line == n, row, spare)
    shard = jnp.concatenate([w_in[0].T, w_out[0], spare], axis=0)

    one, two = (lax.ppermute(shard, COLUMN, home_to_work(flip)) for flip in (0, 1))
    chunk = jnp.concatenate(
        [
            one[:own],
            two[:own],
            one[own : 2 * own],
            two[own : 2 * own],
            one[2 * own : 2 * own + 1],
            two[2 * own : 2 * own + 1],
            jnp.zeros((LINES - 2, chan), bf16),
        ],
        axis=0,
    )
    chunk, x_rows = lax.optimization_barrier((chunk, checkpoints[0]))
    x_rows = lax.ppermute(x_rows, COLUMN, home_to_work(0))
    chunks = [chunk] + [lax.ppermute(chunk, PLANE, along(1, k)) for k in range(1, SIDE)]
    quarter = jnp.concatenate(
        [part[: 4 * own] for part in chunks] + [part[4 * own :] for part in chunks], axis=0
    )
    quarter, x_rows = lax.optimization_barrier((quarter, x_rows))
    gain_row = one[2 * own + 1 : 2 * own + 4].astype(f32)
    gain_row = gain_row[0:1] + gain_row[1:2] + gain_row[2:3]
    near = [quarter] + [lax.ppermute(quarter, PLANE, along(2, k)) for k in ORDER]
    cotangent, near[1] = lax.optimization_barrier((cotangent, near[1]))
    cot_rows = lax.ppermute(
        cotangent, COLUMN, [pair for pair in home_to_work(0) if pair[0] >> 4 == 3]
    )

    width = half // 2
    entry = jnp.arange(chan, dtype=jnp.int32)[:, None]
    hidden_col = jnp.arange(width, dtype=jnp.int32)[None, :]
    select = (
        (entry % own == hidden_col % own) & (entry // own % SAMPLES == sample)
    ).astype(bf16)

    flops = 2 * rows * half * chan
    activate = kernel(
        activation_kernel,
        [
            ((width, chan), bf16),
            ((width, chan), bf16),
            ((rows, chan), bf16),
            ((rows, width), bf16),
            ((rows, width), f32),
        ],
        flops,
    )
    first_far = [across_cores(block) for block in near[:2]]
    first = [activate(x_rows, gain_row, select, *blocks) for blocks in (near[:2], first_far)]
    last_near, cot_rows, *first = lax.optimization_barrier((near[3], cot_rows, *first))
    near, last_far = [near[2], last_near], [across_cores(near[2]), across_cores(last_near)]
    second = [activate(x_rows, gain_row, select, *blocks) for blocks in (near, last_far)]
    quarters = [first[0], second[0], first[1], second[1]]
    normed = quarters[0][2]
    hiddens = [quarter[3] for quarter in quarters]
    held = [x_rows, gain_row]
    for w_in_rows, w_out_rows, _, _, slope in quarters:
        held += [w_in_rows, w_out_rows, slope]

    turn = kernel(turn_kernel, [((rows, chan), bf16)], 4 * flops)
    grad, earlier = cot_rows, jnp.zeros_like(cot_rows)
    for _ in range(3):
        earlier = earlier + grad
        grad = lax.ppermute(turn(grad, *held), "z", next_section())

    far_out, kept = kernel(
        first_outer_kernel, [((half, chan), bf16), ((rows, chan), bf16)], flops
    )(*hiddens[2:], earlier, grad)
    kept, far_out = lax.optimization_barrier((kept, far_out))
    recv_out = across_cores(far_out)
    last_turn = kernel(
        last_turn_kernel,
        [((rows, chan), bf16), ((1, chan), f32)] + [((rows, width), bf16)] * 4,
        4 * flops,
    )
    grad_in, gain_part, pg_0, pg_1, *pg_far = last_turn(kept, *held)
    far_in = kernel(outer_kernel, [((half, chan), bf16)], flops)(*pg_far, normed)
    far_in, recv_out = lax.optimization_barrier((far_in, recv_out))
    recv_in = across_cores(far_in)
    gain_there = across_cores(gain_part)
    sums = kernel(near_kernel, [((SIDE * 4 * own + PAD, chan), bf16)] * SIDE, 2 * flops)(
        pg_0, pg_1, normed, recv_in, *hiddens[:2], kept, recv_out, gain_part, gain_there
    )
    grad_home = lax.ppermute(grad_in, COLUMN, work_to_home(0))
    grad_home = kernel(copy_kernel, [((rows, chan), bf16)])(grad_home)

    parts = [sums[0]] + [
        lax.ppermute(part, PLANE, along(2, SIDE - k)) for k, part in zip(ORDER, sums[1:])
    ]
    *parts, grad_home = lax.optimization_barrier((*parts, grad_home))
    sums = kernel(stage_sum_kernel, [((4 * own + PAD, chan), bf16)] * SIDE)(*parts)
    parts = [sums[0]] + [
        lax.ppermute(part, PLANE, along(1, SIDE - k)) for k, part in enumerate(sums[1:], 1)
    ]
    total = sum(part.astype(f32) for part in parts)
    gain_lines = list(two_parts(total[4 * own : 4 * own + 1] + total[4 * own + 1 : 4 * own + 2]))
    gain_lines.append(jnp.zeros((6, chan), bf16))
    total = total.astype(bf16)
    parts = [
        lax.ppermute(
            jnp.concatenate(
                [
                    total[flip * own : (flip + 1) * own],
                    total[(2 + flip) * own : (3 + flip) * own],
                    *gain_lines,
                ],
                axis=0,
            ),
            COLUMN,
            work_to_home(flip),
        )
        for flip in (1, 0)
    ]
    w_in_home, w_out_home, gain_home = kernel(
        home_kernel, [((own, chan), f32), ((own, chan), f32), ((1, chan), f32)]
    )(*parts)
    return grad_home[None], w_in_home.T[None], w_out_home[None], gain_home


def solution(mesh):
    fine = Mesh(mesh.devices.reshape(2, 2, 4, 8, 2), ALL)
    section, fsdp = ("yl", "core"), ("x", "z", "yh")
    in_specs = (
        P(section, fsdp, None),
        P(fsdp, None),
        P(section, None),
        P(section, None, fsdp),
        P(section, fsdp, None),
        P(section, None, fsdp),
        P(section, None, fsdp),
        P(),
        P(),
    )
    out_specs = (
        P(section, fsdp, None),
        P(section, None, fsdp),
        P(section, fsdp, None),
        P(section, None),
    )
    return jax.shard_map(
        on_device, mesh=fine, in_specs=in_specs, out_specs=out_specs, check_vma=False
    )
```
